32 devices in a mesh: row: 16 (over z, y, x), col: 2 (over core).
Axes of the slice: x: 2, y: 2, z: 4, core: 2. Of those that a mesh axis runs over, the one named last changes fastest.
Arguments:
- c_left: float32 [16, 2, 2048, 256], P('row', 'col'), may hold values from -6 to 6
- c_right: float32 [16, 2, 2048, 256], P('row', 'col'), may hold values from -6 to 6
- c_rank: int32 [16, 2], P('row', 'col'), may hold values from 32 to 256, as said below
- a_left: bfloat16 [16, 2, 2048, 256], P('row', None, 'col'), may hold values from -6 to 6
- a_right: bfloat16 [16, 2, 2048, 256], P('row', None, 'col'), may hold values from -0.125 to 0.125
- a_rank: int32 [16, 2], P('row'), may hold values from 32 to 256, as said below
- a_pattern: int32 [16, 2], P('row'), may hold values 0 or 1
- b_left: bfloat16 [2, 2, 2048, 256], P(None, 'col', 'row'), may hold values from -6 to 6
- b_right: bfloat16 [2, 2, 2048, 256], P(None, 'col', 'row'), may hold values from -0.375 to 0.375
- b_rank: int32 [2, 2], P(None, 'col'), may hold values from 32 to 256, as said below
- b_pattern: int32 [2, 2], P(None, 'col'), may hold values 0 or 1
- probe: bfloat16 [2, 2048, 256], replicated, may hold values from -6 to 6
- target: int32 [16, 2, 2], P('row', 'col'), may hold values from 16 to 240, as said below
Outputs:
- out_left: float32 [16, 2, 2048, 256], P('row', 'col')
- out_right: float32 [16, 2, 2048, 256], P('row', 'col')
The draws below stay inside these ranges and needn't reach their ends.
Inputs may be any that keep to these rules, and one draw needn't show every extreme that they name: `c_rank`: every rank lies from 32 to 256; both ends are taken by some tile. `a_rank`: every rank lies from 32 to 256; both ends are taken by some tile. `b_rank`: every rank lies from 32 to 256; both ends are taken by some tile. With g(r) = max(8, r // 16): target[i, j, 0] <= c_rank[i, j] - g(c_rank[i, j]) and target[i, j, k] <= target[i, j, k - 1] - g(target[i, j, k - 1]); both ends are taken by some tile.
All inputs are finite; a program needn't handle non-finite values. No bound on the sum of `a_pattern` or of `b_pattern` on one device may be relied on, other than what follows from the above.
Results may differ from the reference program's by a relative error of at most 0.0009.
Values may be sent and summed in bfloat16 or wider, within the bound.
No kernel may reach another device: no remote copies, remote signals or barrier semaphores. Data moves between devices by JAX's collectives and lax.ppermute only.
A program may use at most 128 MiB of HBM per device.

```python
import math
import jax
import jax.numpy as jnp
from jax import lax

NB = 2048
R = 256
RMIN = 32
KS = 2
MT = 16
NT = 2


def ranks_with_ends(key, count):
    first, second = jax.random.split(key)
    values = jax.random.randint(first, (count,), RMIN, R + 1)
    order = jax.random.permutation(second, count)
    places = jnp.arange(count)
    values = jnp.where(places == order[0], R, values)
    values = jnp.where(places == order[1], RMIN, values)
    return (values, order)


def margin_of(ranks):
    return jnp.maximum(RMIN // 4, ranks // 16)


def rank_table(key):
    base = jax.random.fold_in(key, 11)
    count = MT * NT
    c_values, order = ranks_with_ends(base, count)
    places = jnp.arange(count)
    columns = []
    previous = c_values
    for step in range(KS):
        step_key = jax.random.fold_in(base, 100 + step)
        lowest = RMIN // 2 + (KS - 1 - step) * (RMIN // 4)
        highest = jnp.maximum(previous - margin_of(previous), lowest)
        chosen = lowest + jax.random.randint(step_key, (count,), 0, highest - lowest + 1)
        chosen = jnp.where(places == order[0], highest, chosen)
        chosen = jnp.where(places == order[1], lowest, chosen)
        columns.append(chosen)
        previous = chosen
    return (c_values.reshape(MT, NT).astype(jnp.int32), jnp.stack(columns, -1).reshape(MT, NT, KS).astype(jnp.int32))


def draw_c_rank(key, part):
    return rank_table(key)[0]


def draw_target(key, part):
    return rank_table(key)[1]


def draw_a_rank(key, part):
    values, order = ranks_with_ends(jax.random.fold_in(key, 23), MT * KS)
    return values.reshape(MT, KS).astype(jnp.int32)


def draw_b_rank(key, part):
    values, order = ranks_with_ends(jax.random.fold_in(key, 37), KS * NT)
    return values.reshape(KS, NT).astype(jnp.int32)


def touch_ends(array, stream_key, least, largest):
    extent = array.shape
    place = [jax.random.randint(jax.random.fold_in(stream_key, axis), (), 0, extent[axis]) for axis in range(len(extent))]
    array = array.at[tuple(place)].set(least)
    longest = extent.index(max(extent))
    place[longest] = (place[longest] + 1) % extent[longest]
    return array.at[tuple(place)].set(largest)


def shard_levels(stream_key, dims, shards, low, top_value):
    level, own = 1.0, jax.random.fold_in(stream_key, 6)
    for axis_at, shards_of in shards:
        draws = jnp.exp(jax.random.uniform(jax.random.fold_in(own, axis_at), (shards_of,), jnp.float32, low / len(shards), top_value / len(shards)))
        level = level * jnp.repeat(draws, dims[axis_at] // shards_of).reshape([-1 if axis == axis_at else 1 for axis in range(len(dims))])
    return level


def noise(stream_key, extent, spread, reach, cuts=(), kind=jnp.bfloat16):
    array = jax.random.normal(stream_key, extent, jnp.float32) * spread
    if len(cuts) > 0:
        array = shard_levels(stream_key, extent, cuts, -0.22, 0.18) * array
    return jnp.clip(array, min=-reach, max=reach).astype(kind)


def setup_inputs(seed: int = 0) -> dict:
    keys = jax.random.split(jax.random.key(seed), 14)
    c_left = noise(keys[0], (MT, NT, NB, R), 1.0, 6.0, ((0, 16), (1, 2)), jnp.float32)
    c_right = noise(keys[1], (MT, NT, NB, R), 1.0, 6.0, ((0, 16), (1, 2)), jnp.float32)
    c_rank = draw_c_rank(jax.random.fold_in(keys[13], 71), 0)
    a_left = noise(keys[3], (MT, KS, NB, R), 1.0, 6.0, ((0, 16), (2, 2)))
    a_right = noise(keys[4], (MT, KS, NB, R), NB ** -0.5, 0.125, ((0, 16), (2, 2)))
    a_rank = draw_a_rank(jax.random.fold_in(keys[13], 71), 0)
    a_pattern = touch_ends((jax.random.randint(keys[6], (MT, KS), 0, 4) < 3).astype(jnp.int32), jax.random.fold_in(keys[6], 1), 0, 1)
    b_left = noise(keys[7], (KS, NT, NB, R), 1.0, 6.0, ((1, 2), (2, 16)))
    b_right = noise(keys[8], (KS, NT, NB, R), R ** -0.5, 0.375, ((1, 2), (2, 16)))
    b_rank = draw_b_rank(jax.random.fold_in(keys[13], 71), 0)
    b_pattern = touch_ends((jax.random.randint(keys[10], (KS, NT), 0, 4) < 3).astype(jnp.int32), jax.random.fold_in(keys[10], 1), 0, 1)
    probe = noise(keys[11], (KS, NB, R), 1.0, 6.0)
    target = draw_target(jax.random.fold_in(keys[13], 71), 0)
    return {"c_left": c_left, "c_right": c_right, "c_rank": c_rank, "a_left": a_left, "a_right": a_right, "a_rank": a_rank, "a_pattern": a_pattern, "b_left": b_left, "b_right": b_right, "b_rank": b_rank, "b_pattern": b_pattern, "probe": probe, "target": target}


def column_mask(count, width):
    return (jnp.arange(width, dtype=jnp.int32) < count).astype(jnp.float32)

def product_of(left, right):
    return jnp.dot(left.astype(jnp.float32), right.astype(jnp.float32), precision=lax.Precision.HIGHEST, preferred_element_type=jnp.float32)

def transposed_product(left, right):
    return lax.dot_general(left.astype(jnp.float32), right.astype(jnp.float32), (((0,), (0,)), ((), ())), precision=lax.Precision.HIGHEST, preferred_element_type=jnp.float32)

def recompress(left, right, keep, extra, extra_right, right_probe, probe_step, tmask):
    tile = left.shape[0]
    probe_cols = probe_step.astype(jnp.float32) * tmask[None, :]
    core_c = transposed_product(right, probe_cols) * keep[:, None]
    core_b = right_probe * tmask[None, :]
    sample = product_of(left, core_c) + product_of(extra, core_b)
    gram = transposed_product(sample, sample) + jnp.diag(1.0 - tmask)
    factor = jnp.linalg.cholesky(gram)
    basis = lax.linalg.triangular_solve(factor, sample, left_side=False, lower=True, transpose_a=True)
    back_c = transposed_product(left, basis) * keep[:, None]
    back_b = transposed_product(extra, basis)
    new_right = (product_of(right, back_c) + product_of(extra_right, back_b)) / math.sqrt(tile)
    return (basis * math.sqrt(tile), new_right)

def reference(c_left, c_right, c_rank, a_left, a_right, a_rank, a_pattern, b_left, b_right, b_rank, b_pattern, probe, target):

    def one_tile(index):
        row_id = index // NT
        col_id = index % NT
        left = c_left[row_id, col_id]
        right = c_right[row_id, col_id]
        keep = column_mask(c_rank[row_id, col_id], R)
        for step in range(KS):
            a_l = a_left[row_id, step]
            a_r = a_right[row_id, step]
            b_l = b_left[step, col_id]
            b_r = b_right[step, col_id]
            weight = (a_pattern[row_id, step] * b_pattern[step, col_id]).astype(jnp.float32)
            middle = lax.dot_general(a_r.astype(jnp.float32), b_l.astype(jnp.float32), (((0,), (0,)), ((), ())), preferred_element_type=jnp.float32)
            middle = middle * column_mask(a_rank[row_id, step], R)[:, None] * column_mask(b_rank[step, col_id], R)[None, :] * weight
            extra = product_of(a_l.astype(jnp.float32), middle)
            right_probe = lax.dot_general(b_r.astype(jnp.float32), probe[step].astype(jnp.float32), (((0,), (0,)), ((), ())), preferred_element_type=jnp.float32)
            tmask = column_mask(target[row_id, col_id, step], R)
            left, right = recompress(left, right, keep, extra, b_r.astype(jnp.float32), right_probe, probe[step], tmask)
            keep = tmask
        return (left, right)
    lefts, rights = lax.map(one_tile, jnp.arange(MT * NT, dtype=jnp.int32))
    return (lefts.reshape(MT, NT, NB, R), rights.reshape(MT, NT, NB, R))
```

```python
import functools
import math

import jax
import jax.numpy as jnp
from jax import lax
from jax.experimental import pallas as pl
from jax.experimental.pallas import tpu as pltpu
from jax.sharding import PartitionSpec as P

F32 = jnp.float32
BF16 = jnp.bfloat16
ANY = pl.ANY
VMEM = pltpu.VMEM
SMEM = pltpu.SMEM
VMEM_LIMIT = 56 * 1024 * 1024
PANEL = 64
CHUNK = 256


def exchange(x, axis, size, bit):
    return lax.ppermute(x, axis, [(r, r ^ bit) for r in range(size)])


def doubled(x, masks, axis, size, bits):
    for bit in bits:
        x = jnp.concatenate([x, exchange(x, axis, size, bit)], axis=0)
        masks = masks + [m ^ bit for m in masks]
    return x, masks


def halves(x, masks, axis, size, bits):
    x, masks = doubled(x, masks, axis, size, bits[:-1])
    other = exchange(x, axis, size, bits[-1])
    return (x, other), (masks, [m ^ bits[-1] for m in masks])


def bits_of(size):
    bits = []
    bit = size // 2
    while bit >= 1:
        bits.append(bit)
        bit //= 2
    return bits


def split2(x):
    high = x.astype(BF16)
    return high, (x - high.astype(F32)).astype(BF16)


def split3(x):
    high = x.astype(BF16)
    rest = x - high.astype(F32)
    mid = rest.astype(BF16)
    return high, mid, (rest - mid.astype(F32)).astype(BF16)


def mm(a, b):
    return lax.dot_general(a, b, (((1,), (0,)), ((), ())), preferred_element_type=F32)


def mm_bt(a, b):
    return lax.dot_general(a, b, (((1,), (1,)), ((), ())), preferred_element_type=F32)


def exact(a, b):
    return lax.dot_general(
        a, b, (((1,), (0,)), ((), ())), precision=lax.Precision.HIGHEST, preferred_element_type=F32
    )


def exact_at(a, b):
    return lax.dot_general(
        a, b, (((0,), (0,)), ((), ())), precision=lax.Precision.HIGHEST, preferred_element_type=F32
    )


def lanes_below(count, rows, width):
    return (lax.broadcasted_iota(jnp.int32, (rows, width), 1) < count).astype(F32)


def rows_below(count, rows, width):
    return (lax.broadcasted_iota(jnp.int32, (rows, width), 0) < count).astype(F32)


def place(srcs, masks, index, dst, sems, first):
    copies = []
    for src, owners in zip(srcs, masks):
        for at, mask in enumerate(owners):
            block = src.at[at]
            rows = block.shape[0]
            start = pl.multiple_of((index ^ mask) * rows, 16)
            copies.append(
                pltpu.make_async_copy(block, dst.at[pl.ds(start, rows), :], sems.at[first + len(copies)])
            )
    return copies


def lane_of(x, at):
    return jnp.broadcast_to(x[:, at : at + 1], (8, 128))


def row_of(x, at):
    return jnp.broadcast_to(x[at : at + 1, :], (8, x.shape[1]))


def factor_panel(rows, first, width):
    count = len(rows)
    lane = lax.broadcasted_iota(jnp.int32, (8, width), 1)
    sub_wide = lax.broadcasted_iota(jnp.int32, (8, width), 0)
    sub = lax.broadcasted_iota(jnp.int32, (8, 128), 0)
    wide = lambda x: jnp.concatenate([x] * (width // 128), 1)
    for s in range(count):
        c0 = first + 8 * s
        col = {}
        for l in range(8):
            for q in range(s, count):
                col[l, q] = lane_of(rows[q], c0 + l)
        inside = (lane >= c0) & (lane < c0 + 8)
        unit = jnp.where(lane == c0 + sub_wide, 1.0, 0.0)
        for q in range(s, count):
            rows[q] = jnp.where(inside, unit if q == s else 0.0, rows[q])
        pivots = jnp.ones((8, 128), F32)
        for l in range(8):
            d = row_of(col[l, s], l)
            inverse = 1.0 / d
            pivots = jnp.where(sub == l, d, pivots)
            mult = {}
            for q in range(s, count):
                mult[q] = col[l, q] * inverse
                if q == s:
                    mult[q] = jnp.where(sub > l, mult[q], 0.0)
            for l2 in range(l + 1, 8):
                e = row_of(col[l, s], l2)
                for q in range(s, count):
                    col[l2, q] = col[l2, q] - mult[q] * e
            pivot_row = row_of(rows[s], l)
            for q in range(s, count):
                rows[q] = rows[q] - wide(mult[q]) * pivot_row
        rows[s] = rows[s] * wide(lax.rsqrt(pivots))
    return rows


def inverse_factor(work):
    n = work.shape[0]
    for p in range(n // PANEL):
        a = p * PANEL
        b = a + PANEL
        rows = [work[a + 8 * i : a + 8 * i + 8, :] for i in range(PANEL // 8)]
        rows = factor_panel(rows, a, n)
        for i in range(PANEL // 8):
            work[a + 8 * i : a + 8 * i + 8, :] = rows[i]
        if b < n:
            full = jnp.concatenate(rows, 0)
            lane = lax.broadcasted_iota(jnp.int32, (PANEL, n), 1)
            row = lax.broadcasted_iota(jnp.int32, (PANEL, n), 0)
            kept = jnp.where((lane > a + row) & (lane < b), 0.0, full)
            base = b // 128 * 128
            update = exact_at(full[:, base:], kept)[b - base :]
            lane = lax.broadcasted_iota(jnp.int32, (n - b, n), 1)
            rest = jnp.where((lane >= a) & (lane < b), 0.0, work[b:, :])
            work[b:, :] = rest - update
    row = lax.broadcasted_iota(jnp.int32, (n, n), 0)
    lane = lax.broadcasted_iota(jnp.int32, (n, n), 1)
    work[...] = jnp.where(lane <= row, work[...], 0.0)


def sample_and_gram(
    tile, width, left_of, a_left, core_c, core_b, tmask_rows, sample_out, gram_out, cross_out
):
    c_h, c_m = split2(core_c)
    b_h, b_m = split2(core_b)
    weights = jnp.concatenate([c_h, c_h, c_m, b_h, b_m], 0)
    hh = jnp.zeros((width, width), F32)
    hm = jnp.zeros((width, width), F32)
    mm_ = jnp.zeros((width, width), F32)
    pc = jnp.zeros((width, width), F32)
    pb = jnp.zeros((width, width), F32)
    for c in range(tile // CHUNK):
        at = slice(c * CHUNK, (c + 1) * CHUNK)
        l_h, l_m = split2(left_of(c))
        al = a_left[at, :]
        part = mm(jnp.concatenate([l_h, l_m, l_h, al, al], 1), weights)
        sample_out[at, :] = part
        s_h, s_m = split2(part)
        t_h = s_h.T
        t_m = s_m.T
        wide = mm(t_h, jnp.concatenate([s_h, s_m, l_h, l_m, al], 1))
        hh += wide[:, :width]
        hm += wide[:, width : 2 * width]
        narrow = mm(t_m, jnp.concatenate([s_m, l_h, al], 1))
        mm_ += narrow[:, :width]
        pc += wide[:, 2 * width : 3 * width] + wide[:, 3 * width : 4 * width] + narrow[:, width : 2 * width]
        pb += wide[:, 4 * width :] + narrow[:, 2 * width :]
    gram_out[...] = hh + hm + hm.T + mm_ + tmask_rows
    cross_out[:, :width] = pc
    cross_out[:, width:] = pb


def unit_beyond(count, width):
    row = lax.broadcasted_iota(jnp.int32, (width, width), 0)
    lane = lax.broadcasted_iota(jnp.int32, (width, width), 1)
    return jnp.where((row == lane) & (row >= count), 1.0, 0.0)


def probe_kernel(steps, right, probe, out, right_v, probe_v, sems):
    tile = right_v.shape[0]
    width = right_v.shape[1]
    copies = [pltpu.make_async_copy(right, right_v, sems.at[0]), pltpu.make_async_copy(probe, probe_v, sems.at[1])]
    for copy in copies:
        copy.start()
    for copy in copies:
        copy.wait()
    total = [jnp.zeros((width, width), F32) for _ in range(steps)]
    for c in range(tile // CHUNK):
        at = slice(c * CHUNK, (c + 1) * CHUNK)
        parts = split3(right_v[at, :])
        stacked = jnp.concatenate([part.T for part in parts], 1)
        for k in range(steps):
            piece = probe_v[k, at, :]
            total[k] += mm(stacked, jnp.concatenate([piece] * 3, 0))
    for k in range(steps):
        out[k] = total[k]


def middle_kernel(
    masks_a, masks_l, masks_r, step, steps, rest, scal, place_at,
    al0, al1, ar0, ar1, bl0, bl1, br0, br1, probe,
    mid_out, rp_out, al_out, br_out,
    ar_v, bl_v, probe_v, sems,
):
    tile, width = ar_v.shape
    col_at = place_at[0]
    row_at = place_at[1]
    copies_ar = place([r.at[:, step] for r in (ar0, ar1)], masks_a, col_at, ar_v, sems, 0)
    n = len(copies_ar)
    copies_bl = place((bl0, bl1), masks_l, row_at, bl_v, sems, n)
    n += len(copies_bl)
    copies_br = place((br0, br1), masks_r, row_at, br_out, sems, n)
    n += len(copies_br)
    copies_al = place([r.at[:, step] for r in (al0, al1)], masks_a, col_at, al_out, sems, n)
    n += len(copies_al)
    copy_probe = pltpu.make_async_copy(probe.at[pl.ds(step, steps - step)], probe_v, sems.at[n])
    for copy in copies_bl + copies_ar + copies_br + [copy_probe] + copies_al:
        copy.start()
    for copy in copies_bl + copies_ar:
        copy.wait()
    mid = lax.dot_general(ar_v[...], bl_v[...], (((0,), (0,)), ((), ())), preferred_element_type=F32)
    a_rank = scal[1 + steps + step]
    b_rank = scal[1 + 2 * steps + step]
    weight = scal[1 + 3 * steps + step].astype(F32)
    mid_out[...] = mid * rows_below(a_rank, width, width) * lanes_below(b_rank, width, width) * weight
    for copy in copies_br + [copy_probe]:
        copy.wait()
    for k in range(steps - step):
        rp_out[k] = lax.dot_general(
            br_out[...], probe_v[k], (((0,), (0,)), ((), ())), preferred_element_type=F32
        )
    for copy in copies_al:
        copy.wait()


def first_kernel(scal, left, al, mid, rp, core, sample_out, gram_out, cross_out, left_v, sems):
    tile, width = left_v.shape
    count = tile // CHUNK
    copies = []
    for c in range(count):
        at = pl.ds(c * CHUNK, CHUNK)
        copies.append(pltpu.make_async_copy(left.at[at, :], left_v.at[at, :], sems.at[c]))
        copies[-1].start()
    tmask = lanes_below(scal[1], width, width)
    core_c = core[...] * rows_below(scal[0], width, width) * tmask
    core_b = exact(mid[...], rp[...] * tmask)

    def left_of(c):
        copies[c].wait()
        return left_v[c * CHUNK : (c + 1) * CHUNK, :]

    sample_and_gram(
        tile, width, left_of, al, core_c, core_b, unit_beyond(scal[1], width), sample_out, gram_out, cross_out
    )


def inverse_kernel(gram, out):
    out[...] = gram[...]
    inverse_factor(out)


def second_kernel(
    scal, sample0, inv0, cross0, mid0, rp01, core1, mid1, rp11, al1, right, br0, br1,
    out_left, out_right, left_v, sample_v, gram_v, cross_v, right_v, br0_v, br1_v, sems,
):
    tile, width = left_v.shape
    root = math.sqrt(tile)
    copies = [
        pltpu.make_async_copy(s, d, sems.at[i])
        for i, (s, d) in enumerate([(right, right_v), (br0, br0_v), (br1, br1_v)])
    ]
    for copy in copies:
        copy.start()
    t0 = scal[1]
    t1 = scal[2]
    w = inv0[...]
    w_h, w_m, w_l = split3(w)
    w_wide = jnp.concatenate([w_h, w_h, w_m, w_m, w_h, w_l], 1)
    for c in range(tile // CHUNK):
        at = slice(c * CHUNK, (c + 1) * CHUNK)
        h, m, l = split3(sample0[at, :])
        left_v[at, :] = mm_bt(jnp.concatenate([h, m, h, m, l, h], 1), w_wide) * root
    bc0 = exact(w, cross0[:, :width]) * lanes_below(scal[0], width, width)
    bb0 = exact(exact(w, cross0[:, width:]), mid0[...])
    core_c = (exact(bc0, core1[...]) + exact(bb0, rp01[...])) * (1.0 / root)
    tmask = lanes_below(t1, width, width)
    core_c = core_c * rows_below(t0, width, width) * tmask
    core_b = exact(mid1[...], rp11[...] * tmask)
    sample_and_gram(
        tile, width, lambda c: left_v[c * CHUNK : (c + 1) * CHUNK, :], al1, core_c, core_b,
        unit_beyond(t1, width), sample_v, gram_v, cross_v,
    )
    inverse_factor(gram_v)
    w = gram_v[...]
    w_h, w_m, w_l = split3(w)
    w_wide = jnp.concatenate([w_h, w_h, w_m, w_m, w_h, w_l], 1)
    for c in range(tile // CHUNK):
        at = slice(c * CHUNK, (c + 1) * CHUNK)
        h, m, l = split3(sample_v[at, :])
        out_left[at, :] = mm_bt(jnp.concatenate([h, m, h, m, l, h], 1), w_wide) * root
    bc1 = exact(w, cross_v[:, :width]) * lanes_below(t0, width, width)
    bb1 = exact(exact(w, cross_v[:, width:]), mid1[...])
    e_h, e_m = split2(exact(bc1, bc0) * (1.0 / tile))
    f_h, f_m = split2(exact(bc1, bb0) * (1.0 / tile))
    g_h, g_m = split2(bb1 * (1.0 / root))
    coef = jnp.concatenate([e_h, e_h, e_m, f_h, f_m, g_h, g_m], 1)
    for copy in copies:
        copy.wait()
    for c in range(tile // CHUNK):
        at = slice(c * CHUNK, (c + 1) * CHUNK)
        h, m = split2(right_v[at, :])
        b0 = br0_v[at, :]
        b1 = br1_v[at, :]
        out_right[at, :] = mm_bt(jnp.concatenate([h, m, h, b0, b0, b1, b1], 1), coef)


def call(kernel, out_shape, in_specs, scratch, name):
    return pl.pallas_call(
        kernel,
        out_shape=out_shape,
        in_specs=in_specs,
        out_specs=jax.tree.map(lambda _: pl.BlockSpec(memory_space=VMEM), out_shape),
        scratch_shapes=scratch,
        compiler_params=pltpu.CompilerParams(vmem_limit_bytes=VMEM_LIMIT),
        name=name,
    )


def on_device(
    rows_count, cols_count, c_left, c_right, c_rank, a_left, a_right, a_rank, a_pattern,
    b_left, b_right, b_rank, b_pattern, probe, target,
):
    tile, width = c_left.shape[2:]
    steps = probe.shape[0]
    left = c_left[0, 0]
    right = c_right[0, 0]
    any_, vm, sm = (pl.BlockSpec(memory_space=s) for s in (ANY, VMEM, SMEM))
    square = jax.ShapeDtypeStruct((width, width), F32)
    dma = pltpu.SemaphoreType.DMA

    scal = jnp.concatenate(
        [c_rank[0], target[0, 0], a_rank[0], b_rank[:, 0], a_pattern[0] * b_pattern[:, 0]]
    ).astype(jnp.int32)
    place_at = jnp.stack([lax.axis_index("col"), lax.axis_index("row")]).astype(jnp.int32)

    a_bits = bits_of(cols_count)
    al_pieces, masks_a = halves(a_left, [0], "col", cols_count, a_bits)
    ar_pieces, _ = halves(a_right, [0], "col", cols_count, a_bits)
    b_bits = bits_of(rows_count)
    pieces = []
    for k in range(steps):
        x = jnp.stack([b_left[k, 0], b_right[k, 0]])[None]
        x, masks = doubled(x, [0], "row", rows_count, b_bits[:-2])
        x_l, masks_l = halves(x[:, 0], masks, "row", rows_count, [b_bits[-1], b_bits[-2]])
        x_r, masks_r = halves(x[:, 1], masks, "row", rows_count, [b_bits[-2], b_bits[-1]])
        pieces.append((x_l, x_r))

    core = call(
        functools.partial(probe_kernel, steps),
        jax.ShapeDtypeStruct((steps, width, width), F32),
        [any_, any_],
        [VMEM((tile, width), F32), VMEM((steps, tile, width), BF16), dma((2,))],
        "right_probe",
    )(right, probe)

    mids, rps, als, brs = [], [], [], []
    for k in range(steps):
        n_sems = 2 * cols_count + 2 * rows_count + 1
        x_l, x_r = pieces[k]
        mid, rp, al, br = call(
            functools.partial(middle_kernel, masks_a, masks_l, masks_r, k, steps, 0),
            (
                square,
                jax.ShapeDtypeStruct((steps - k, width, width), F32),
                jax.ShapeDtypeStruct((tile, width), BF16),
                jax.ShapeDtypeStruct((tile, width), BF16),
            ),
            [sm, sm] + [any_] * 9,
            [
                VMEM((tile, width), BF16),
                VMEM((tile, width), BF16),
                VMEM((steps - k, tile, width), BF16),
                dma((n_sems,)),
            ],
            "middle",
        )(scal, place_at, *al_pieces, *ar_pieces, *x_l, *x_r, probe)
        mids.append(mid)
        rps.append(rp)
        als.append(al)
        brs.append(br)

    sample, gram, cross = call(
        first_kernel,
        (
            jax.ShapeDtypeStruct((tile, width), F32),
            square,
            jax.ShapeDtypeStruct((width, 2 * width), F32),
        ),
        [sm, any_] + [vm] * 4,
        [VMEM((tile, width), F32), dma((tile // CHUNK,))],
        "sample",
    )(scal, left, als[0], mids[0], rps[0][0], core[0])
    inverse = call(inverse_kernel, square, [vm], [], "inverse_factor")(gram)
    full = jax.ShapeDtypeStruct((tile, width), F32)
    out_left, out_right = call(
        second_kernel,
        (full, full),
        [sm] + [vm] * 9 + [any_] * 3,
        [
            VMEM((tile, width), F32),
            VMEM((tile, width), F32),
            VMEM((width, width), F32),
            VMEM((width, 2 * width), F32),
            VMEM((tile, width), F32),
            VMEM((tile, width), BF16),
            VMEM((tile, width), BF16),
            dma((3,)),
        ],
        "second_step",
    )(scal, sample, inverse, cross, mids[0], rps[0][1], core[1], mids[1], rps[1][0], als[1], right, brs[0], brs[1])
    return (out_left[None, None], out_right[None, None])


def solution(mesh):
    return jax.shard_map(
        functools.partial(on_device, mesh.shape["row"], mesh.shape["col"]),
        mesh=mesh,
        in_specs=(
            P("row", "col", None, None),
            P("row", "col", None, None),
            P("row", "col"),
            P("row", None, "col", None),
            P("row", None, "col", None),
            P("row", None),
            P("row", None),
            P(None, "col", "row", None),
            P(None, "col", "row", None),
            P(None, "col"),
            P(None, "col"),
            P(),
            P("row", "col", None),
        ),
        out_specs=(P("row", "col", None, None), P("row", "col", None, None)),
        check_vma=False,
    )
```

```python
import functools
import math

import jax
import jax.numpy as jnp
from jax import lax
from jax.experimental import pallas as pl
from jax.experimental.pallas import tpu as pltpu
from jax.sharding import PartitionSpec as P

F32 = jnp.float32
BF16 = jnp.bfloat16
ANY = pl.ANY
VMEM = pltpu.VMEM
SMEM = pltpu.SMEM
PANEL = 64
CHUNK = 256


def exchange(x, axis, size, bit):
    return lax.ppermute(x, axis, [(r, r ^ bit) for r in range(size)])


def doubled(x, masks, axis, size, bits):
    for bit in bits:
        x = jnp.concatenate([x, exchange(x, axis, size, bit)], axis=0)
        masks = masks + [m ^ bit for m in masks]
    return x, masks


def halves(x, masks, axis, size, bits):
    x, masks = doubled(x, masks, axis, size, bits[:-1])
    other = exchange(x, axis, size, bits[-1])
    return (x, other), (masks, [m ^ bits[-1] for m in masks])


def bits_of(size):
    bits = []
    bit = size // 2
    while bit >= 1:
        bits.append(bit)
        bit //= 2
    return bits


def split2(x):
    high = x.astype(BF16)
    return high, (x - high.astype(F32)).astype(BF16)


def mm(a, b):
    return lax.dot_general(a, b, (((1,), (0,)), ((), ())), preferred_element_type=F32)


def mm_at(a, b):
    return lax.dot_general(a, b, (((0,), (0,)), ((), ())), preferred_element_type=F32)


def exact_bt(a, b):
    return lax.dot_general(
        a, b, (((1,), (1,)), ((), ())), precision=lax.Precision.HIGHEST, preferred_element_type=F32
    )


def exact(a, b):
    return lax.dot_general(
        a, b, (((1,), (0,)), ((), ())), precision=lax.Precision.HIGHEST, preferred_element_type=F32
    )


def exact_at(a, b):
    return lax.dot_general(
        a, b, (((0,), (0,)), ((), ())), precision=lax.Precision.HIGHEST, preferred_element_type=F32
    )


def lanes_below(count, rows, width):
    return (lax.broadcasted_iota(jnp.int32, (rows, width), 1) < count).astype(F32)


def rows_below(count, rows, width):
    return (lax.broadcasted_iota(jnp.int32, (rows, width), 0) < count).astype(F32)


def place(srcs, masks, index, dst, sems, first):
    copies = []
    for src, owners in zip(srcs, masks):
        for at, mask in enumerate(owners):
            block = src.at[at]
            rows = block.shape[0]
            start = pl.multiple_of((index ^ mask) * rows, 16)
            copies.append(
                pltpu.make_async_copy(block, dst.at[pl.ds(start, rows), :], sems.at[first + len(copies)])
            )
    return copies


def lane_of(x, at):
    return jnp.broadcast_to(x[:, at : at + 1], (8, 128))


def row_of(x, at):
    return jnp.broadcast_to(x[at : at + 1, :], (8, x.shape[1]))


def factor_panel(rows, first, width):
    count = len(rows)
    lane = lax.broadcasted_iota(jnp.int32, (8, width), 1)
    sub_wide = lax.broadcasted_iota(jnp.int32, (8, width), 0)
    sub = lax.broadcasted_iota(jnp.int32, (8, 128), 0)
    wide = lambda x: jnp.concatenate([x] * (width // 128), 1)
    for s in range(count):
        c0 = first + 8 * s
        col = {}
        for l in range(8):
            for q in range(s, count):
                col[l, q] = lane_of(rows[q], c0 + l)
        inside = (lane >= c0) & (lane < c0 + 8)
        unit = jnp.where(lane == c0 + sub_wide, 1.0, 0.0)
        for q in range(s, count):
            rows[q] = jnp.where(inside, unit if q == s else 0.0, rows[q])
        pivots = jnp.ones((8, 128), F32)
        for l in range(8):
            d = row_of(col[l, s], l)
            inverse = 1.0 / d
            pivots = jnp.where(sub == l, d, pivots)
            mult = {}
            for q in range(s, count):
                mult[q] = col[l, q] * inverse
                if q == s:
                    mult[q] = jnp.where(sub > l, mult[q], 0.0)
            for l2 in range(l + 1, 8):
                e = row_of(col[l, s], l2)
                for q in range(s, count):
                    col[l2, q] = col[l2, q] - mult[q] * e
            pivot_row = row_of(rows[s], l)
            for q in range(s, count):
                rows[q] = rows[q] - wide(mult[q]) * pivot_row
        rows[s] = rows[s] * wide(lax.rsqrt(pivots))
    return rows


def inverse_factor(work):
    n = work.shape[0]
    for p in range(n // PANEL):
        a = p * PANEL
        b = a + PANEL
        rows = [work[a + 8 * i : a + 8 * i + 8, :] for i in range(PANEL // 8)]
        rows = factor_panel(rows, a, n)
        for i in range(PANEL // 8):
            work[a + 8 * i : a + 8 * i + 8, :] = rows[i]
        if b < n:
            full = jnp.concatenate(rows, 0)
            lane = lax.broadcasted_iota(jnp.int32, (PANEL, n), 1)
            row = lax.broadcasted_iota(jnp.int32, (PANEL, n), 0)
            kept = jnp.where((lane > a + row) & (lane < b), 0.0, full)
            base = b // 128 * 128
            update = exact_at(full[:, base:], kept)[b - base :]
            lane = lax.broadcasted_iota(jnp.int32, (n - b, n), 1)
            rest = jnp.where((lane >= a) & (lane < b), 0.0, work[b:, :])
            work[b:, :] = rest - update
    row = lax.broadcasted_iota(jnp.int32, (n, n), 0)
    lane = lax.broadcasted_iota(jnp.int32, (n, n), 1)
    work[...] = jnp.where(lane <= row, work[...], 0.0)


def unit_beyond(count, width):
    row = lax.broadcasted_iota(jnp.int32, (width, width), 0)
    lane = lax.broadcasted_iota(jnp.int32, (width, width), 1)
    return jnp.where((row == lane) & (row >= count), 1.0, 0.0)


def probe_kernel(steps, right, probe, out, right_v, probe_v, sems):
    tile, width = right_v.shape
    copies = [pltpu.make_async_copy(right, right_v, sems.at[0])]
    for k in range(steps):
        here = probe_v.at[:, pl.ds(k * width, width)]
        copies.append(pltpu.make_async_copy(probe.at[k], here, sems.at[1 + k]))
    for copy in copies:
        copy.start()
    for copy in copies:
        copy.wait()
    high, mid = split2(right_v[...])
    both = probe_v[...]
    total = mm_at(high, both) + mm_at(mid, both)
    for k in range(steps):
        out[k] = total[:, k * width : (k + 1) * width]


def cross_kernel(masks_a, steps, scal, left, al0, al1, out, left_v, parts_v, sems):
    tile, width = left_v.shape
    copy_left = pltpu.make_async_copy(left, left_v, sems.at[0])
    copies = []
    for k in range(steps):
        here = parts_v.at[:, pl.ds((2 + k) * width, width)]
        copies += place([r.at[:, k] for r in (al0, al1)], masks_a, scal[1 + 4 * steps], here, sems, 1 + len(copies))
    copy_left.start()
    for copy in copies:
        copy.start()
    copy_left.wait()
    high, mid = split2(left_v[...])
    parts_v[:, :width] = high
    parts_v[:, width : 2 * width] = mid
    for copy in copies:
        copy.wait()
    x = mm_at(parts_v[:, :width], parts_v[...])
    y = mm_at(parts_v[:, width : 2 * width], parts_v[:, width:])
    hm = x[:, width : 2 * width]
    out[:width, :width] = x[:, :width] + hm + hm.T + y[:, :width]
    la = x[:, 2 * width :] + y[:, width:]
    out[:width, width:] = la
    out[width:, :width] = la.T
    out[width:, width:] = mm_at(parts_v[:, 2 * width :], parts_v[:, 2 * width :])


def middle_of(scal, step, steps, ar_v, bl_v):
    width = ar_v.shape[1]
    mid = mm_at(ar_v[...], bl_v[...])
    weight = scal[1 + 3 * steps + step].astype(F32)
    a_rank, b_rank = scal[1 + steps + step], scal[1 + 2 * steps + step]
    return mid * rows_below(a_rank, width, width) * lanes_below(b_rank, width, width) * weight


def first_kernel(
    masks_a, masks_l, masks_r, steps, scal, ar0, ar1, bl0, bl1, br0, br1, probe, core, cross,
    mid_out, rp_out, k_out, y_out, w_out, ar_v, bl_v, br_v, probe_v, sems,
):
    tile, width = ar_v.shape
    col_at, row_at = scal[1 + 4 * steps], scal[2 + 4 * steps]
    copies = place([r.at[:, 0] for r in (ar0, ar1)], masks_a, col_at, ar_v, sems, 0)
    copies += place((bl0, bl1), masks_l, row_at, bl_v, sems, len(copies))
    late = place((br0, br1), masks_r, row_at, br_v, sems, len(copies))
    for k in range(steps):
        here = probe_v.at[:, pl.ds(k * width, width)]
        late.append(pltpu.make_async_copy(probe.at[k], here, sems.at[len(copies) + len(late)]))
    for copy in copies + late:
        copy.start()
    tmask = lanes_below(scal[1], width, width)
    k_out[:width, :] = core[0] * rows_below(scal[0], width, width) * tmask
    for copy in copies:
        copy.wait()
    mid = middle_of(scal, 0, steps, ar_v, bl_v)
    mid_out[...] = mid
    for copy in late:
        copy.wait()
    rp = mm_at(br_v[...], probe_v[...])
    rp_out[...] = rp[:, width:]
    k_out[width:, :] = exact(mid, rp[:, :width] * tmask)
    k = k_out[...]
    y = exact(cross[: 2 * width, : 2 * width], k)
    y_out[...] = y
    w_out[...] = exact_at(k, y) + unit_beyond(scal[1], width)
    inverse_factor(w_out)


def second_kernel(
    masks_a, masks_l, masks_r, steps, scal, k0, y0, w0, mid0, rp01, core, cross, probe, left, right,
    al0, al1, ar0, ar1, bl0, bl1, br0, br1, brp0, brp1,
    out_left, out_right,
    left_v, right_v, a_v, b_v, ar_v, bl_v, probe_v, gram_v, outl_v, outr_v, sems, out_sems,
):
    tile, width = ar_v.shape
    root = math.sqrt(tile)
    col_at, row_at = scal[1 + 4 * steps], scal[2 + 4 * steps]
    soon = place([r.at[:, 1] for r in (ar0, ar1)], masks_a, col_at, ar_v, sems, 0)
    soon += place((bl0, bl1), masks_l, row_at, bl_v, sems, len(soon))
    soon += place((br0, br1), masks_r, row_at, b_v.at[:, pl.ds(width, width)], sems, len(soon))
    soon.append(pltpu.make_async_copy(probe.at[1], probe_v, sems.at[len(soon)]))
    n = len(soon)
    late = place((brp0, brp1), masks_r, row_at, b_v.at[:, pl.ds(0, width)], sems, n)
    for k in range(steps):
        here = a_v.at[:, pl.ds(k * width, width)]
        late += place([r.at[:, k] for r in (al0, al1)], masks_a, col_at, here, sems, n + len(late))
    late.append(pltpu.make_async_copy(left, left_v, sems.at[n + len(late)]))
    late.append(pltpu.make_async_copy(right, right_v, sems.at[n + len(late)]))
    for copy in soon + late:
        copy.start()
    t0, t1 = scal[1], scal[2]
    mid0_ = mid0[...]
    z = exact_bt(jnp.concatenate([k0[...], y0[...]], 0), w0[...])
    v0 = z[: 2 * width] * root
    back_c0 = z[2 * width : 3 * width] * rows_below(scal[0], width, width)
    back_b0 = exact_at(mid0_, z[3 * width :])
    back0 = jnp.concatenate([back_c0, back_b0], 0)
    tmask = lanes_below(t1, width, width)
    core_c = exact_at(back0, jnp.concatenate([core[1], rp01[...]], 0)) * (1.0 / root)
    core_c = core_c * rows_below(t0, width, width) * tmask
    for copy in soon:
        copy.wait()
    mid1 = middle_of(scal, 1, steps, ar_v, bl_v)
    rp11 = mm_at(b_v[:, width:], probe_v[...])
    core_b = exact(mid1, rp11 * tmask)
    k1 = jnp.concatenate([exact(v0, core_c), core_b], 0)
    y1 = exact(cross[...], k1)
    gram_v[...] = exact_at(k1, y1) + unit_beyond(t1, width)
    cross_c = exact_at(v0, y1[: 2 * width])
    inverse_factor(gram_v)
    z = exact_bt(jnp.concatenate([k1, cross_c, y1[2 * width :]], 0), gram_v[...])
    back_c1 = z[3 * width : 4 * width] * rows_below(t0, width, width)
    back_b1 = exact_at(mid1, z[4 * width :])
    h, m = split2(z[: 3 * width] * root)
    w_left = jnp.concatenate([h[:width], h[:width], m[:width], h[width:], m[width:]], 0)
    for copy in late:
        copy.wait()
    outs = []

    def send(src, dst, c):
        at = pl.ds(c * CHUNK, CHUNK)
        copy = pltpu.make_async_copy(src.at[at, :], dst.at[at, :], out_sems.at[len(outs)])
        copy.start()
        outs.append(copy)

    for c in range(tile // CHUNK):
        at = slice(c * CHUNK, (c + 1) * CHUNK)
        h, m = split2(left_v[at, :])
        a = a_v[at, :]
        outl_v[at, :] = mm(jnp.concatenate([h, m, h, a, a], 1), w_left)
        send(outl_v, out_left, c)
    first = exact(back0, back_c1) * (1.0 / tile)
    h, m = split2(jnp.concatenate([first, back_b1 * (1.0 / root)], 0))
    w_right = jnp.concatenate([h[:width], h[:width], m[:width], h[width:], m[width:]], 0)
    for c in range(tile // CHUNK):
        at = slice(c * CHUNK, (c + 1) * CHUNK)
        h, m = split2(right_v[at, :])
        b = b_v[at, :]
        outr_v[at, :] = mm(jnp.concatenate([h, m, h, b, b], 1), w_right)
        send(outr_v, out_right, c)
    for copy in outs:
        copy.wait()


def call(kernel, out_shape, in_specs, scratch, name, vmem, passes, out_space=VMEM):
    flops = passes * 2 * 2048 * 256 * 256
    return pl.pallas_call(
        kernel,
        out_shape=out_shape,
        in_specs=in_specs,
        out_specs=jax.tree.map(lambda _: pl.BlockSpec(memory_space=out_space), out_shape),
        scratch_shapes=scratch,
        compiler_params=pltpu.CompilerParams(vmem_limit_bytes=vmem * 1024 * 1024),
        cost_estimate=pl.CostEstimate(flops=flops, bytes_accessed=1 << 20, transcendentals=0),
        name=name,
    )


def on_device(
    rows_count, cols_count, c_left, c_right, c_rank, a_left, a_right, a_rank, a_pattern,
    b_left, b_right, b_rank, b_pattern, probe, target,
):
    tile, width = c_left.shape[2:]
    steps = probe.shape[0]
    left = c_left[0, 0]
    right = c_right[0, 0]
    any_, vm, sm = (pl.BlockSpec(memory_space=s) for s in (ANY, VMEM, SMEM))
    dma = pltpu.SemaphoreType.DMA

    def f32(*shape):
        return jax.ShapeDtypeStruct(shape, F32)

    scal = jnp.concatenate(
        [
            c_rank[0],
            target[0, 0],
            a_rank[0],
            b_rank[:, 0],
            a_pattern[0] * b_pattern[:, 0],
            jnp.stack([lax.axis_index("col"), lax.axis_index("row")]),
        ]
    ).astype(jnp.int32)

    a_bits = bits_of(cols_count)
    al, masks_a = halves(a_left, [0], "col", cols_count, a_bits)
    ar, _ = halves(a_right, [0], "col", cols_count, a_bits)
    b_bits = bits_of(rows_count)
    bl, br = [], []
    for k in range(steps):
        x = jnp.stack([b_left[k, 0], b_right[k, 0]])[None]
        x, masks = doubled(x, [0], "row", rows_count, b_bits[:-2])
        x_l, masks_l = halves(x[:, 0], masks, "row", rows_count, [b_bits[-1], b_bits[-2]])
        x_r, masks_r = halves(x[:, 1], masks, "row", rows_count, [b_bits[-2], b_bits[-1]])
        bl.append(x_l)
        br.append(x_r)

    core = call(
        functools.partial(probe_kernel, steps),
        f32(steps, width, width),
        [any_, any_],
        [VMEM((tile, width), F32), VMEM((tile, steps * width), BF16), dma((1 + steps,))],
        "right_probe",
        16,
        12,
    )(right, probe)
    cross = call(
        functools.partial(cross_kernel, masks_a, steps),
        f32((1 + steps) * width, (1 + steps) * width),
        [sm] + [any_] * 3,
        [VMEM((tile, width), F32), VMEM((tile, (2 + steps) * width), BF16), dma((1 + steps * cols_count,))],
        "left_cross",
        24,
        24,
    )(scal, left, *al)

    part = VMEM((tile, width), BF16)
    whole = VMEM((tile, width), F32)
    wide = VMEM((tile, steps * width), BF16)
    mid0, rp01, k0, y0, w0 = call(
        functools.partial(first_kernel, masks_a, masks_l, masks_r, steps),
        (f32(width, width), f32(width, width), f32(2 * width, width), f32(2 * width, width), f32(width, width)),
        [sm] + [any_] * 7 + [vm] * 2,
        [part, part, part, wide, dma((cols_count + 2 * rows_count + steps,))],
        "first_step",
        24,
        50,
    )(scal, *ar, *bl[0], *br[0], probe, core, cross)
    out_left, out_right = call(
        functools.partial(second_kernel, masks_a, masks_l, masks_r, steps),
        (f32(tile, width), f32(tile, width)),
        [sm] + [vm] * 7 + [any_] * 13,
        [
            whole, whole, wide, wide, part, part, part, VMEM((width, width), F32), whole, whole,
            dma(((1 + steps) * cols_count + 3 * rows_count + 3,)), dma((2 * (tile // CHUNK),)),
        ],
        "second_step",
        40,
        100,
        ANY,
    )(scal, k0, y0, w0, mid0, rp01, core, cross, probe, left, right, *al, *ar, *bl[1], *br[1], *br[0])
    return (out_left[None, None], out_right[None, None])


def solution(mesh):
    return jax.shard_map(
        functools.partial(on_device, mesh.shape["row"], mesh.shape["col"]),
        mesh=mesh,
        in_specs=(
            P("row", "col", None, None),
            P("row", "col", None, None),
            P("row", "col"),
            P("row", None, "col", None),
            P("row", None, "col", None),
            P("row", None),
            P("row", None),
            P(None, "col", "row", None),
            P(None, "col", "row", None),
            P(None, "col"),
            P(None, "col"),
            P(),
            P("row", "col", None),
        ),
        out_specs=(P("row", "col", None, None), P("row", "col", None, None)),
        check_vma=False,
    )
```

```python
import functools
import math

import jax
import jax.numpy as jnp
from jax import lax
from jax.experimental import pallas as pl
from jax.experimental.pallas import tpu as pltpu
from jax.sharding import PartitionSpec as P

F32 = jnp.float32
BF16 = jnp.bfloat16
ANY = pl.ANY
VMEM = pltpu.VMEM
SMEM = pltpu.SMEM
PANEL = 64
CHUNK = 256


def exchange(x, axis, size, bit):
    return lax.ppermute(x, axis, [(r, r ^ bit) for r in range(size)])


def spread(x, axis, size, bits):
    blocks, masks = [x], [0]
    for bit in bits:
        blocks += [exchange(block, axis, size, bit) for block in blocks]
        masks += [mask ^ bit for mask in masks]
    return blocks, masks


def after(x, *before):
    return lax.optimization_barrier((x, *before))[0]


def bits_of(size):
    bits = []
    bit = size // 2
    while bit >= 1:
        bits.append(bit)
        bit //= 2
    return bits


def split2(x):
    high = x.astype(BF16)
    return high, (x - high.astype(F32)).astype(BF16)


def mm(a, b):
    return lax.dot_general(a, b, (((1,), (0,)), ((), ())), preferred_element_type=F32)


def mm_at(a, b):
    return lax.dot_general(a, b, (((0,), (0,)), ((), ())), preferred_element_type=F32)


def exact_bt(a, b):
    return lax.dot_general(
        a, b, (((1,), (1,)), ((), ())), precision=lax.Precision.HIGHEST, preferred_element_type=F32
    )


def exact(a, b):
    return lax.dot_general(
        a, b, (((1,), (0,)), ((), ())), precision=lax.Precision.HIGHEST, preferred_element_type=F32
    )


def exact_at(a, b):
    return lax.dot_general(
        a, b, (((0,), (0,)), ((), ())), precision=lax.Precision.HIGHEST, preferred_element_type=F32
    )


def lanes_below(count, rows, width):
    return (lax.broadcasted_iota(jnp.int32, (rows, width), 1) < count).astype(F32)


def rows_below(count, rows, width):
    return (lax.broadcasted_iota(jnp.int32, (rows, width), 0) < count).astype(F32)


def place(srcs, masks, index, dst, sems, first):
    copies = []
    for src, owners in zip(srcs, masks):
        for at, mask in enumerate(owners):
            block = src.at[at]
            rows = block.shape[0]
            start = pl.multiple_of((index ^ mask) * rows, 16)
            copies.append(
                pltpu.make_async_copy(block, dst.at[pl.ds(start, rows), :], sems.at[first + len(copies)])
            )
    return copies


def lane_of(x, at):
    return jnp.broadcast_to(x[:, at : at + 1], (8, 128))


def row_of(x, at):
    return jnp.broadcast_to(x[at : at + 1, :], (8, x.shape[1]))


def factor_panel(rows, first, width):
    count = len(rows)
    lane = lax.broadcasted_iota(jnp.int32, (8, width), 1)
    sub_wide = lax.broadcasted_iota(jnp.int32, (8, width), 0)
    sub = lax.broadcasted_iota(jnp.int32, (8, 128), 0)
    wide = lambda x: jnp.concatenate([x] * (width // 128), 1)
    for s in range(count):
        c0 = first + 8 * s
        col = {}
        for l in range(8):
            for q in range(s, count):
                col[l, q] = lane_of(rows[q], c0 + l)
        inside = (lane >= c0) & (lane < c0 + 8)
        unit = jnp.where(lane == c0 + sub_wide, 1.0, 0.0)
        for q in range(s, count):
            rows[q] = jnp.where(inside, unit if q == s else 0.0, rows[q])
        pivots = jnp.ones((8, 128), F32)
        for l in range(8):
            d = row_of(col[l, s], l)
            inverse = 1.0 / d
            pivots = jnp.where(sub == l, d, pivots)
            mult = {}
            for q in range(s, count):
                mult[q] = col[l, q] * inverse
                if q == s:
                    mult[q] = jnp.where(sub > l, mult[q], 0.0)
            for l2 in range(l + 1, 8):
                e = row_of(col[l, s], l2)
                for q in range(s, count):
                    col[l2, q] = col[l2, q] - mult[q] * e
            pivot_row = row_of(rows[s], l)
            for q in range(s, count):
                rows[q] = rows[q] - wide(mult[q]) * pivot_row
        rows[s] = rows[s] * wide(lax.rsqrt(pivots))
    return rows


def inverse_factor(work):
    n = work.shape[0]
    for p in range(n // PANEL):
        a = p * PANEL
        b = a + PANEL
        rows = [work[a + 8 * i : a + 8 * i + 8, :] for i in range(PANEL // 8)]
        rows = factor_panel(rows, a, n)
        for i in range(PANEL // 8):
            work[a + 8 * i : a + 8 * i + 8, :] = rows[i]
        if b < n:
            full = jnp.concatenate(rows, 0)
            lane = lax.broadcasted_iota(jnp.int32, (PANEL, n), 1)
            row = lax.broadcasted_iota(jnp.int32, (PANEL, n), 0)
            kept = jnp.where((lane > a + row) & (lane < b), 0.0, full)
            base = b // 128 * 128
            update = exact_at(full[:, base:], kept)[b - base :]
            lane = lax.broadcasted_iota(jnp.int32, (n - b, n), 1)
            rest = jnp.where((lane >= a) & (lane < b), 0.0, work[b:, :])
            work[b:, :] = rest - update
    row = lax.broadcasted_iota(jnp.int32, (n, n), 0)
    lane = lax.broadcasted_iota(jnp.int32, (n, n), 1)
    work[...] = jnp.where(lane <= row, work[...], 0.0)


def unit_beyond(count, width):
    row = lax.broadcasted_iota(jnp.int32, (width, width), 0)
    lane = lax.broadcasted_iota(jnp.int32, (width, width), 1)
    return jnp.where((row == lane) & (row >= count), 1.0, 0.0)


def probe_kernel(steps, right, probe, out, right_v, probe_v, sems):
    tile, width = right_v.shape
    copies = [pltpu.make_async_copy(right, right_v, sems.at[0])]
    for k in range(steps):
        here = probe_v.at[:, pl.ds(k * width, width)]
        copies.append(pltpu.make_async_copy(probe.at[k], here, sems.at[1 + k]))
    for copy in copies:
        copy.start()
    for copy in copies:
        copy.wait()
    high, mid = split2(right_v[...])
    both = probe_v[...]
    total = mm_at(high, both) + mm_at(mid, both)
    for k in range(steps):
        out[k] = total[:, k * width : (k + 1) * width]


def cross_kernel(masks_a, steps, scal, left, *refs):
    al, (out, left_v, parts_v, sems) = refs[: len(masks_a)], refs[len(masks_a) :]
    tile, width = left_v.shape
    copy_left = pltpu.make_async_copy(left, left_v, sems.at[0])
    copies = []
    for k in range(steps):
        here = parts_v.at[:, pl.ds((2 + k) * width, width)]
        copies += place([r.at[:, k] for r in al], masks_a, scal[1 + 4 * steps], here, sems, 1 + len(copies))
    copy_left.start()
    for copy in copies:
        copy.start()
    copy_left.wait()
    high, mid = split2(left_v[...])
    parts_v[:, :width] = high
    parts_v[:, width : 2 * width] = mid
    for copy in copies:
        copy.wait()
    x = mm_at(parts_v[:, :width], parts_v[...])
    y = mm_at(parts_v[:, width : 2 * width], parts_v[:, width:])
    hm = x[:, width : 2 * width]
    out[:width, :width] = x[:, :width] + hm + hm.T + y[:, :width]
    la = x[:, 2 * width :] + y[:, width:]
    out[:width, width:] = la
    out[width:, :width] = la.T
    out[width:, width:] = mm_at(parts_v[:, 2 * width :], parts_v[:, 2 * width :])


def middle_of(scal, step, steps, ar_v, bl_v):
    width = ar_v.shape[1]
    mid = mm_at(ar_v[...], bl_v[...])
    weight = scal[1 + 3 * steps + step].astype(F32)
    a_rank, b_rank = scal[1 + steps + step], scal[1 + 2 * steps + step]
    return mid * rows_below(a_rank, width, width) * lanes_below(b_rank, width, width) * weight


def first_kernel(
    masks_a, masks_b, steps, scal, *refs
):
    ar, refs = refs[: len(masks_a)], refs[len(masks_a) :]
    b0, b1, b2, bl3, br3, probe, core, cross, mid_out, rp_out, k_out, y_out, gram_out = refs[:13]
    ar_v, bl_v, br_v, probe_v, sems = refs[13:]
    tile, width = ar_v.shape
    col_at, row_at = scal[1 + 4 * steps], scal[2 + 4 * steps]
    copies = place([r.at[:, 0] for r in ar], masks_a, col_at, ar_v, sems, 0)
    copies += place((b0.at[0], b1.at[0], b2.at[0], bl3), masks_b, row_at, bl_v, sems, len(copies))
    late = place((b0.at[1], b1.at[1], b2.at[1], br3), masks_b, row_at, br_v, sems, len(copies))
    for k in range(steps):
        here = probe_v.at[:, pl.ds(k * width, width)]
        late.append(pltpu.make_async_copy(probe.at[k], here, sems.at[len(copies) + len(late)]))
    for copy in copies + late:
        copy.start()
    tmask = lanes_below(scal[1], width, width)
    k_out[:width, :] = core[0] * rows_below(scal[0], width, width) * tmask
    for copy in copies:
        copy.wait()
    mid = middle_of(scal, 0, steps, ar_v, bl_v)
    mid_out[...] = mid
    for copy in late:
        copy.wait()
    rp = mm_at(br_v[...], probe_v[...])
    rp_out[...] = rp[:, width:]
    k_out[width:, :] = exact(mid, rp[:, :width] * tmask)
    k = k_out[...]
    y = exact(cross[: 2 * width, : 2 * width], k)
    y_out[...] = y
    gram_out[...] = exact_at(k, y) + unit_beyond(scal[1], width)


def inverse_kernel(gram, out):
    out[...] = gram[...]
    inverse_factor(out)


def second_kernel(
    masks_a, masks_b, steps, scal, k0, y0, w0, mid0, rp01, core, cross, probe, left, right,
    *refs,
):
    n = len(masks_a)
    al, ar, refs = refs[:n], refs[n : 2 * n], refs[2 * n :]
    b0, b1, b2, bl3, br3, p0, p1, p2, pr3, out_left, out_right = refs[:11]
    left_v, right_v, a_v, b_v, ar_v, bl_v, probe_v, gram_v, outl_v, outr_v, sems, out_sems = refs[11:]
    tile, width = ar_v.shape
    root = math.sqrt(tile)
    col_at, row_at = scal[1 + 4 * steps], scal[2 + 4 * steps]
    soon = place([r.at[:, 1] for r in ar], masks_a, col_at, ar_v, sems, 0)
    soon += place((b0.at[0], b1.at[0], b2.at[0], bl3), masks_b, row_at, bl_v, sems, len(soon))
    here = b_v.at[:, pl.ds(width, width)]
    soon += place((b0.at[1], b1.at[1], b2.at[1], br3), masks_b, row_at, here, sems, len(soon))
    soon.append(pltpu.make_async_copy(probe.at[1], probe_v, sems.at[len(soon)]))
    n = len(soon)
    here = b_v.at[:, pl.ds(0, width)]
    late = place((p0.at[1], p1.at[1], p2.at[1], pr3), masks_b, row_at, here, sems, n)
    for k in range(steps):
        here = a_v.at[:, pl.ds(k * width, width)]
        late += place([r.at[:, k] for r in al], masks_a, col_at, here, sems, n + len(late))
    late.append(pltpu.make_async_copy(left, left_v, sems.at[n + len(late)]))
    late.append(pltpu.make_async_copy(right, right_v, sems.at[n + len(late)]))
    for copy in soon + late:
        copy.start()
    t0, t1 = scal[1], scal[2]
    mid0_ = mid0[...]
    z = exact_bt(jnp.concatenate([k0[...], y0[...]], 0), w0[...])
    v0 = z[: 2 * width] * root
    back_c0 = z[2 * width : 3 * width] * rows_below(scal[0], width, width)
    back_b0 = exact_at(mid0_, z[3 * width :])
    back0 = jnp.concatenate([back_c0, back_b0], 0)
    tmask = lanes_below(t1, width, width)
    core_c = exact_at(back0, jnp.concatenate([core[1], rp01[...]], 0)) * (1.0 / root)
    core_c = core_c * rows_below(t0, width, width) * tmask
    for copy in soon:
        copy.wait()
    mid1 = middle_of(scal, 1, steps, ar_v, bl_v)
    rp11 = mm_at(b_v[:, width:], probe_v[...])
    core_b = exact(mid1, rp11 * tmask)
    k1 = jnp.concatenate([exact(v0, core_c), core_b], 0)
    y1 = exact(cross[...], k1)
    gram_v[...] = exact_at(k1, y1) + unit_beyond(t1, width)
    cross_c = exact_at(v0, y1[: 2 * width])
    inverse_factor(gram_v)
    z = exact_bt(jnp.concatenate([k1, cross_c, y1[2 * width :]], 0), gram_v[...])
    back_c1 = z[3 * width : 4 * width] * rows_below(t0, width, width)
    back_b1 = exact_at(mid1, z[4 * width :])
    h, m = split2(z[: 3 * width] * root)
    w_left = jnp.concatenate([h[:width], h[:width], m[:width], h[width:], m[width:]], 0)
    for copy in late:
        copy.wait()
    outs = []

    def send(src, dst, c):
        at = pl.ds(c * CHUNK, CHUNK)
        copy = pltpu.make_async_copy(src.at[at, :], dst.at[at, :], out_sems.at[len(outs)])
        copy.start()
        outs.append(copy)

    for c in range(tile // CHUNK):
        at = slice(c * CHUNK, (c + 1) * CHUNK)
        h, m = split2(left_v[at, :])
        a = a_v[at, :]
        outl_v[at, :] = mm(jnp.concatenate([h, m, h, a, a], 1), w_left)
        send(outl_v, out_left, c)
    first = exact(back0, back_c1) * (1.0 / tile)
    h, m = split2(jnp.concatenate([first, back_b1 * (1.0 / root)], 0))
    w_right = jnp.concatenate([h[:width], h[:width], m[:width], h[width:], m[width:]], 0)
    for c in range(tile // CHUNK):
        at = slice(c * CHUNK, (c + 1) * CHUNK)
        h, m = split2(right_v[at, :])
        b = b_v[at, :]
        outr_v[at, :] = mm(jnp.concatenate([h, m, h, b, b], 1), w_right)
        send(outr_v, out_right, c)
    for copy in outs:
        copy.wait()


def call(kernel, out_shape, in_specs, scratch, name, vmem, passes, out_space=VMEM):
    flops = passes * 2 * 2048 * 256 * 256
    return pl.pallas_call(
        kernel,
        out_shape=out_shape,
        in_specs=in_specs,
        out_specs=jax.tree.map(lambda _: pl.BlockSpec(memory_space=out_space), out_shape),
        scratch_shapes=scratch,
        compiler_params=pltpu.CompilerParams(vmem_limit_bytes=vmem * 1024 * 1024),
        cost_estimate=pl.CostEstimate(flops=flops, bytes_accessed=1 << 20, transcendentals=0),
        name=name,
    )


def on_device(
    rows_count, cols_count, c_left, c_right, c_rank, a_left, a_right, a_rank, a_pattern,
    b_left, b_right, b_rank, b_pattern, probe, target,
):
    tile, width = c_left.shape[2:]
    steps = probe.shape[0]
    left = c_left[0, 0]
    right = c_right[0, 0]
    any_, vm, sm = (pl.BlockSpec(memory_space=s) for s in (ANY, VMEM, SMEM))
    dma = pltpu.SemaphoreType.DMA

    def f32(*shape):
        return jax.ShapeDtypeStruct(shape, F32)

    scal = jnp.concatenate(
        [
            c_rank[0],
            target[0, 0],
            a_rank[0],
            b_rank[:, 0],
            a_pattern[0] * b_pattern[:, 0],
            jnp.stack([lax.axis_index("col"), lax.axis_index("row")]),
        ]
    ).astype(jnp.int32)

    a_bits = bits_of(cols_count)
    al, masks = spread(a_left, "col", cols_count, a_bits)
    ar, _ = spread(a_right, "col", cols_count, a_bits)
    masks_a = [[mask] for mask in masks]
    bits = bits_of(rows_count)
    one, two = bits[-1], bits[-2]
    core = call(
        functools.partial(probe_kernel, steps),
        f32(steps, width, width),
        [any_, any_],
        [VMEM((tile, width), F32), VMEM((tile, steps * width), BF16), dma((1 + steps,))],
        "right_probe",
        16,
        12,
    )(right, probe)
    cross = call(
        functools.partial(cross_kernel, masks_a, steps),
        f32((1 + steps) * width, (1 + steps) * width),
        [sm] + [any_] * (1 + cols_count),
        [VMEM((tile, width), F32), VMEM((tile, (2 + steps) * width), BF16), dma((1 + steps * cols_count,))],
        "left_cross",
        24,
        24,
    )(scal, left, *al)

    gathered = []
    for k in range(steps):
        x = jnp.stack([b_left[k, 0], b_right[k, 0]])[:, None]
        if k > 0:
            x = after(x, gathered[k - 1][0])
        blocks, masks = spread(x, "row", rows_count, bits[:-2])
        x = jnp.concatenate(blocks, 1)
        x = after(x, *gathered[k - 1][3:]) if k > 0 else after(x, core, al[-1])
        x1 = exchange(x, "row", rows_count, one)
        x2 = exchange(x, "row", rows_count, two)
        l3 = exchange(after(x1[0], cross), "row", rows_count, two)
        r3 = exchange(after(x2[1], cross), "row", rows_count, one)
        gathered.append((x, x1, x2, l3, r3))
    masks_b = [[mask ^ flip for mask in masks] for flip in (0, one, two, one ^ two)]

    part = VMEM((tile, width), BF16)
    whole = VMEM((tile, width), F32)
    wide = VMEM((tile, steps * width), BF16)
    mid0, rp01, k0, y0, gram = call(
        functools.partial(first_kernel, masks_a, masks_b, steps),
        (f32(width, width), f32(width, width), f32(2 * width, width), f32(2 * width, width), f32(width, width)),
        [sm] + [any_] * (cols_count + 6) + [vm] * 2,
        [part, part, part, wide, dma((cols_count + 2 * rows_count + steps,))],
        "first_step",
        24,
        20,
    )(scal, *ar, *gathered[0], probe, core, cross)
    w0 = call(inverse_kernel, f32(width, width), [vm], [], "inverse_factor", 16, 30)(gram)
    x, x1, x2, l3, r3 = gathered[0]
    out_left, out_right = call(
        functools.partial(second_kernel, masks_a, masks_b, steps),
        (f32(tile, width), f32(tile, width)),
        [sm] + [vm] * 7 + [any_] * (3 + 2 * cols_count + 9),
        [
            whole, whole, wide, wide, part, part, part, VMEM((width, width), F32), whole, whole,
            dma(((1 + steps) * cols_count + 3 * rows_count + 3,)), dma((2 * (tile // CHUNK),)),
        ],
        "second_step",
        40,
        100,
        ANY,
    )(scal, k0, y0, w0, mid0, rp01, core, cross, probe, left, right, *al, *ar, *gathered[1], x, x1, x2, r3)
    return (out_left[None, None], out_right[None, None])


def solution(mesh):
    return jax.shard_map(
        functools.partial(on_device, mesh.shape["row"], mesh.shape["col"]),
        mesh=mesh,
        in_specs=(
            P("row", "col", None, None),
            P("row", "col", None, None),
            P("row", "col"),
            P("row", None, "col", None),
            P("row", None, "col", None),
            P("row", None),
            P("row", None),
            P(None, "col", "row", None),
            P(None, "col", "row", None),
            P(None, "col"),
            P(None, "col"),
            P(),
            P("row", "col", None),
        ),
        out_specs=(P("row", "col", None, None), P("row", "col", None, None)),
        check_vma=False,
    )
```

```python
import functools
import math

import jax
import jax.numpy as jnp
from jax import lax
from jax.experimental import pallas as pl
from jax.experimental.pallas import tpu as pltpu
from jax.sharding import PartitionSpec as P

F32 = jnp.float32
BF16 = jnp.bfloat16
ANY = pl.ANY
VMEM = pltpu.VMEM
SMEM = pltpu.SMEM
PANEL = 64
CHUNK = 256


def exchange(x, axis, size, bit):
    return lax.ppermute(x, axis, [(r, r ^ bit) for r in range(size)])


def spread(x, axis, size, bits):
    masks = [0]
    for bit in bits:
        masks += [mask ^ bit for mask in masks]
    masks = sorted(masks, reverse=True)[:-1]
    return [x] + [exchange(x, axis, size, mask) for mask in masks], [0] + masks


def forwarded(x, axis, size, bits):
    blocks, masks = [x], [0]
    for bit in bits:
        blocks += [exchange(block, axis, size, bit) for block in blocks]
        masks += [mask ^ bit for mask in masks]
    return blocks, masks


def after(x, *before):
    return lax.optimization_barrier((x, *before))[0]


def bits_of(size):
    bits = []
    bit = size // 2
    while bit >= 1:
        bits.append(bit)
        bit //= 2
    return bits


def split2(x):
    high = x.astype(BF16)
    return high, (x - high.astype(F32)).astype(BF16)


def mm(a, b):
    return lax.dot_general(a, b, (((1,), (0,)), ((), ())), preferred_element_type=F32)


def mm_at(a, b):
    return lax.dot_general(a, b, (((0,), (0,)), ((), ())), preferred_element_type=F32)


def mm_bt(a, b):
    return lax.dot_general(a, b, (((1,), (1,)), ((), ())), preferred_element_type=F32)


def close(a, b):
    a_h, a_m = split2(a)
    b_h, b_m = split2(b)
    return mm(jnp.concatenate([a_h, a_m, a_h], 1), jnp.concatenate([b_h, b_h, b_m], 0))


def close_at(a, b):
    a_h, a_m = split2(a)
    b_h, b_m = split2(b)
    return mm_at(jnp.concatenate([a_h, a_m, a_h], 0), jnp.concatenate([b_h, b_h, b_m], 0))


def close_bt(a, b):
    a_h, a_m = split2(a)
    b_h, b_m = split2(b)
    return mm_bt(jnp.concatenate([a_h, a_m, a_h], 1), jnp.concatenate([b_h, b_h, b_m], 1))


def exact(a, b):
    return lax.dot_general(
        a, b, (((1,), (0,)), ((), ())), precision=lax.Precision.HIGHEST, preferred_element_type=F32
    )


def exact_at(a, b):
    return lax.dot_general(
        a, b, (((0,), (0,)), ((), ())), precision=lax.Precision.HIGHEST, preferred_element_type=F32
    )


def lanes_below(count, rows, width):
    return (lax.broadcasted_iota(jnp.int32, (rows, width), 1) < count).astype(F32)


def rows_below(count, rows, width):
    return (lax.broadcasted_iota(jnp.int32, (rows, width), 0) < count).astype(F32)


def place(srcs, masks, index, dst, sems, first):
    copies = []
    for src, owners in zip(srcs, masks):
        for at, mask in enumerate(owners):
            block = src.at[at]
            rows = block.shape[0]
            start = pl.multiple_of((index ^ mask) * rows, 16)
            copies.append(
                pltpu.make_async_copy(block, dst.at[pl.ds(start, rows), :], sems.at[first + len(copies)])
            )
    return copies


def lane_of(x, at):
    return jnp.broadcast_to(x[:, at : at + 1], (8, 128))


def row_of(x, at):
    return jnp.broadcast_to(x[at : at + 1, :], (8, x.shape[1]))


def factor_panel(rows, first, width, between):
    count = len(rows)
    lane = lax.broadcasted_iota(jnp.int32, (8, width), 1)
    sub_wide = lax.broadcasted_iota(jnp.int32, (8, width), 0)
    sub = lax.broadcasted_iota(jnp.int32, (8, 128), 0)
    wide = lambda x: jnp.concatenate([x] * (width // 128), 1)
    for s in range(count):
        c0 = first + 8 * s
        col = {}
        for l in range(8):
            for q in range(s, count):
                col[l, q] = lane_of(rows[q], c0 + l)
        inside = (lane >= c0) & (lane < c0 + 8)
        unit = jnp.where(lane == c0 + sub_wide, 1.0, 0.0)
        for q in range(s, count):
            rows[q] = jnp.where(inside, unit if q == s else 0.0, rows[q])
        pivots = jnp.ones((8, 128), F32)
        for l in range(8):
            d = row_of(col[l, s], l)
            inverse = 1.0 / d
            pivots = jnp.where(sub == l, d, pivots)
            mult = {}
            for q in range(s, count):
                mult[q] = col[l, q] * inverse
                if q == s:
                    mult[q] = jnp.where(sub > l, mult[q], 0.0)
            for l2 in range(l + 1, 8):
                e = row_of(col[l, s], l2)
                for q in range(s, count):
                    col[l2, q] = col[l2, q] - mult[q] * e
            pivot_row = row_of(rows[s], l)
            for q in range(s, count):
                rows[q] = rows[q] - wide(mult[q]) * pivot_row
        rows[s] = rows[s] * wide(lax.rsqrt(pivots))
        between(c0 // 8)
    return rows


def inverse_factor(work, beside=()):
    n = work.shape[0]
    beside = list(beside)
    slots = n // PANEL
    for p in range(slots):
        a = p * PANEL
        b = a + PANEL
        rows = [work[a + 8 * i : a + 8 * i + 8, :] for i in range(PANEL // 8)]
        rows = factor_panel(rows, a, n, functools.partial(some_of, beside, n // 8))
        for i in range(PANEL // 8):
            work[a + 8 * i : a + 8 * i + 8, :] = rows[i]
        if b < n:
            full = jnp.concatenate(rows, 0)
            lane = lax.broadcasted_iota(jnp.int32, (PANEL, n), 1)
            row = lax.broadcasted_iota(jnp.int32, (PANEL, n), 0)
            kept = jnp.where((lane > a + row) & (lane < b), 0.0, full)
            base = b // 128 * 128
            update = exact_at(full[:, base:], kept)[b - base :]
            lane = lax.broadcasted_iota(jnp.int32, (n - b, n), 1)
            rest = jnp.where((lane >= a) & (lane < b), 0.0, work[b:, :])
            work[b:, :] = rest - update
    while beside:
        beside.pop(0)()
    row = lax.broadcasted_iota(jnp.int32, (n, n), 0)
    lane = lax.broadcasted_iota(jnp.int32, (n, n), 1)
    work[...] = jnp.where(lane <= row, work[...], 0.0)


def some_of(beside, slabs, slab):
    for _ in range(-(-len(beside) // (slabs - slab))):
        beside.pop(0)()


def unit_beyond(count, width):
    row = lax.broadcasted_iota(jnp.int32, (width, width), 0)
    lane = lax.broadcasted_iota(jnp.int32, (width, width), 1)
    return jnp.where((row == lane) & (row >= count), 1.0, 0.0)


def probe_kernel(steps, right, probe, out, right_v, probe_v, sems):
    tile, width = right_v.shape
    copies = [pltpu.make_async_copy(right, right_v, sems.at[0])]
    for k in range(steps):
        here = probe_v.at[:, pl.ds(k * width, width)]
        copies.append(pltpu.make_async_copy(probe.at[k], here, sems.at[1 + k]))
    for copy in copies:
        copy.start()
    for copy in copies:
        copy.wait()
    high, mid = split2(right_v[...])
    both = probe_v[...]
    total = mm_at(high, both) + mm_at(mid, both)
    for k in range(steps):
        out[k] = total[:, k * width : (k + 1) * width]


def cross_kernel(masks_a, steps, scal, left, *refs):
    al, (out, left_v, parts_v, sems) = refs[: len(masks_a)], refs[len(masks_a) :]
    tile, width = left_v.shape
    copy_left = pltpu.make_async_copy(left, left_v, sems.at[0])
    copies = []
    for k in range(steps):
        here = parts_v.at[:, pl.ds((2 + k) * width, width)]
        copies += place([r.at[:, k] for r in al], masks_a, scal[1 + 4 * steps], here, sems, 1 + len(copies))
    copy_left.start()
    for copy in copies:
        copy.start()
    copy_left.wait()
    high, mid = split2(left_v[...])
    parts_v[:, :width] = high
    parts_v[:, width : 2 * width] = mid
    for copy in copies:
        copy.wait()
    x = mm_at(parts_v[:, :width], parts_v[...])
    y = mm_at(parts_v[:, width : 2 * width], parts_v[:, width:])
    hm = x[:, width : 2 * width]
    out[:width, :width] = x[:, :width] + hm + hm.T + y[:, :width]
    la = x[:, 2 * width :] + y[:, width:]
    out[:width, width:] = la
    out[width:, :width] = la.T
    out[width:, width:] = mm_at(parts_v[:, 2 * width :], parts_v[:, 2 * width :])


def order_kernel(masks_a, masks_b, steps, scal, probe, *refs):
    ar, (ar_out, probe_out, ar_v, probe_v, sems) = refs[: len(masks_a)], refs[len(masks_a) :]
    col_at, row_at = scal[1 + 4 * steps], scal[2 + 4 * steps]
    copies = []
    for k in range(steps):
        here = pl.ds(k * ar_v.shape[1] // steps, ar_v.shape[1] // steps)
        copies += place([r.at[:, k] for r in ar], masks_a, col_at, ar_v.at[:, here], sems, len(copies))
        copies.append(pltpu.make_async_copy(probe.at[k], probe_v.at[:, here], sems.at[len(copies)]))
    for copy in copies:
        copy.start()
    for copy in copies:
        copy.wait()
    masks = sum(masks_b, [])
    rows = ar_v.shape[0] // len(masks)
    for at, mask in enumerate(masks):
        start = pl.multiple_of((row_at ^ mask) * rows, 16)
        ar_out[at * rows : (at + 1) * rows, :] = ar_v[pl.ds(start, rows), :]
        probe_out[at * rows : (at + 1) * rows, :] = probe_v[pl.ds(start, rows), :]


def summed(lefts, rights):
    total = None
    for left, right in zip(lefts, rights):
        part = mm_at(left, right)
        total = part if total is None else total + part
    return total


def pieces_of(refs, which):
    x, x1, x2, l3, r3 = refs
    n, rows, width = l3.shape
    return [r[...].reshape(n * rows, width) for r in (x.at[which], x1.at[which], x2.at[which], (l3, r3)[which])]


def quarters(ref, k, width):
    rows = ref.shape[0] // 4
    return [ref[i * rows : (i + 1) * rows, k * width : (k + 1) * width] for i in range(4)]


def middle_of(scal, step, steps, ar, b):
    width = ar.shape[1] // steps
    mid = summed(quarters(ar, step, width), pieces_of(b, 0))
    weight = scal[1 + 3 * steps + step].astype(F32)
    a_rank, b_rank = scal[1 + steps + step], scal[1 + 2 * steps + step]
    return mid * rows_below(a_rank, width, width) * lanes_below(b_rank, width, width) * weight


def first_kernel(steps, scal, ar, probe, *refs):
    b, (core, cross, mid_out, rp_out, k_out, y_out, gram_out) = refs[:5], refs[5:]
    width = mid_out.shape[0]
    tmask = lanes_below(scal[1], width, width)
    k_out[:width, :] = core[0] * rows_below(scal[0], width, width) * tmask
    mid = middle_of(scal, 0, steps, ar, b)
    mid_out[...] = mid
    rows = probe.shape[0] // 4
    rp = summed(pieces_of(b, 1), [probe[i * rows : (i + 1) * rows, :] for i in range(4)])
    rp_out[...] = rp[:, width:]
    k_out[width:, :] = exact(mid, rp[:, :width] * tmask)
    k = k_out[...]
    y = exact(cross[: 2 * width, : 2 * width], k)
    y_out[...] = y
    gram_out[...] = exact_at(k, y) + unit_beyond(scal[1], width)


def inverse_kernel(tile, scal, gram, k0, y0, cross, mid0, rp01, core, w_out, core_out, h_out, t_v):
    width = gram.shape[0]
    root = math.sqrt(tile)
    w_out[...] = gram[...]

    def next_core():
        y = jnp.concatenate([y0[:width, :] * rows_below(scal[0], width, width), y0[width:, :]], 0)
        z = jnp.concatenate([core[1], exact(mid0[...], rp01[...])], 0)
        t_v[:, :width] = exact_at(y, z) * (1.0 / root)

    def next_cross():
        t_v[:, width:] = exact(cross[2 * width :, : 2 * width], k0[...]).T * root

    inverse_factor(w_out, [next_core, next_cross])
    both = exact(w_out[...], t_v[...])
    keep = rows_below(scal[1], width, width)
    core_out[...] = both[:, :width] * keep * lanes_below(scal[2], width, width)
    h_out[...] = both[:, width:] * keep


def second_kernel(
    masks_a, masks_b, steps, scal, k0, y0, w0, core_c, h0, mid0, cross, ar, probe, *refs,
):
    n = len(masks_a)
    b, refs = refs[:5], refs[5:]
    left, right, b0, b1, b2, br3, p0, p1, p2, pr3 = refs[:10]
    al, refs = refs[10 : 10 + n], refs[10 + n :]
    out_left, out_right = refs[:2]
    left_v, right_v, a_v, b_v, gram_v, k_v, q_v, outl_v, outr_v, sems, out_sems = refs[2:]
    tile, width = left_v.shape
    root = math.sqrt(tile)
    col_at, row_at = scal[1 + 4 * steps], scal[2 + 4 * steps]
    late = []
    for k, (x, x1, x2, r3) in enumerate(((p0, p1, p2, pr3), (b0, b1, b2, br3))):
        here = pl.ds(k * width, width)
        late += place((x.at[1], x1.at[1], x2.at[1], r3), masks_b, row_at, b_v.at[:, here], sems, len(late))
        late += place([r.at[:, k] for r in al], masks_a, col_at, a_v.at[:, here], sems, len(late))
    late.append(pltpu.make_async_copy(left, left_v, sems.at[len(late)]))
    late.append(pltpu.make_async_copy(right, right_v, sems.at[len(late)]))
    for copy in late:
        copy.start()
    t0, t1 = scal[1], scal[2]
    a = core_c[...]
    h = h0[...]
    h_a = exact_at(h, a)
    mid1 = middle_of(scal, 1, steps, ar, b)
    rp11 = summed(pieces_of(b, 1), quarters(probe, 1, width))
    core_b = exact(mid1, rp11 * lanes_below(t1, width, width))
    both = exact(jnp.concatenate([h, cross[2 * width :, 2 * width :]], 0), core_b)
    top = a * float(tile) + both[:width]
    low = h_a + both[width:]
    gram_v[...] = exact_at(jnp.concatenate([a, core_b], 0), jnp.concatenate([top, low], 0)) + unit_beyond(t1, width)

    def left_weights():
        k_c = close(k0[...], close_at(w0[...], a) * root)
        h, m = split2(jnp.concatenate([k_c, core_b], 0))
        k_v[...] = jnp.concatenate([h[:width], h[:width], m[:width], h[width:], m[width:]], 0)

    def right_weights():
        z = close_bt(y0[...], w0[...])
        back0 = jnp.concatenate([z[:width] * rows_below(scal[0], width, width), close_at(mid0[...], z[width:])], 0)
        q_c = close(back0, top * rows_below(t0, width, width)) * (1.0 / tile)
        h, m = split2(jnp.concatenate([q_c, close_at(mid1, low) * (1.0 / root)], 0))
        q_v[...] = jnp.concatenate([h[:width], h[:width], m[:width], h[width:], m[width:]], 0)

    def arrive():
        for copy in late:
            copy.wait()

    def form(out_v, factor, others, weights, c):
        at = slice(c * CHUNK, (c + 1) * CHUNK)
        h, m = split2(factor[at, :])
        o = others[at, :]
        out_v[at, :] = mm(jnp.concatenate([h, m, h, o, o], 1), weights[...])

    count = tile // CHUNK
    beside = [left_weights, right_weights, arrive]
    beside += [functools.partial(form, outl_v, left_v, a_v, k_v, c) for c in range(count)]
    beside += [functools.partial(form, outr_v, right_v, b_v, q_v, c) for c in range(count)]
    inverse_factor(gram_v, beside)
    h, m = split2(gram_v[...])
    weights = jnp.concatenate([h, h, m], 1)
    outs = []
    for c in range(count):
        at = pl.ds(c * CHUNK, CHUNK)
        for src, dst, scale in ((outl_v, out_left, root), (outr_v, out_right, 1.0)):
            h, m = split2(src[at, :])
            src[at, :] = mm_bt(jnp.concatenate([h, m, h], 1), weights) * scale
            copy = pltpu.make_async_copy(src.at[at, :], dst.at[at, :], out_sems.at[len(outs)])
            copy.start()
            outs.append(copy)
    for copy in outs:
        copy.wait()


def call(kernel, out_shape, in_specs, scratch, name, vmem, passes, out_space=VMEM):
    flops = passes * 2 * 2048 * 256 * 256
    return pl.pallas_call(
        kernel,
        out_shape=out_shape,
        in_specs=in_specs,
        out_specs=jax.tree.map(lambda _: pl.BlockSpec(memory_space=out_space), out_shape),
        scratch_shapes=scratch,
        compiler_params=pltpu.CompilerParams(vmem_limit_bytes=vmem * 1024 * 1024),
        cost_estimate=pl.CostEstimate(flops=flops, bytes_accessed=1 << 20, transcendentals=0),
        name=name,
    )


def on_device(
    rows_count, cols_count, c_left, c_right, c_rank, a_left, a_right, a_rank, a_pattern,
    b_left, b_right, b_rank, b_pattern, probe, target,
):
    tile, width = c_left.shape[2:]
    steps = probe.shape[0]
    left = c_left[0, 0]
    right = c_right[0, 0]
    any_, vm, sm = (pl.BlockSpec(memory_space=s) for s in (ANY, VMEM, SMEM))
    dma = pltpu.SemaphoreType.DMA

    def f32(*shape):
        return jax.ShapeDtypeStruct(shape, F32)

    scal = jnp.concatenate(
        [
            c_rank[0],
            target[0, 0],
            a_rank[0],
            b_rank[:, 0],
            a_pattern[0] * b_pattern[:, 0],
            jnp.stack([lax.axis_index("col"), lax.axis_index("row")]),
        ]
    ).astype(jnp.int32)

    whole = VMEM((tile, width), F32)
    wide = VMEM((tile, steps * width), BF16)
    a_bits = bits_of(cols_count)
    al, masks = spread(a_left, "col", cols_count, a_bits)
    ar, _ = spread(a_right, "col", cols_count, a_bits)
    masks_a = [[mask] for mask in masks]
    bits = bits_of(rows_count)
    one, two = bits[-1], bits[-2]
    core = call(
        functools.partial(probe_kernel, steps),
        f32(steps, width, width),
        [any_, any_],
        [VMEM((tile, width), F32), VMEM((tile, steps * width), BF16), dma((1 + steps,))],
        "right_probe",
        16,
        12,
    )(right, probe)
    cross = call(
        functools.partial(cross_kernel, masks_a, steps),
        f32((1 + steps) * width, (1 + steps) * width),
        [sm] + [any_] * (1 + cols_count),
        [VMEM((tile, width), F32), VMEM((tile, (2 + steps) * width), BF16), dma((1 + steps * cols_count,))],
        "left_cross",
        24,
        24,
    )(scal, left, *al)

    def own_blocks(k, *before):
        x = jnp.stack([b_left[k, 0], b_right[k, 0]])[:, None]
        return (forwarded if True else spread)(after(x, *before) if before else x, "row", rows_count, bits[:-2])

    blocks, masks = own_blocks(0)
    masks_b = [[mask ^ flip for mask in masks] for flip in (0, one, two, one ^ two)]
    ordered = call(
        functools.partial(order_kernel, masks_a, masks_b, steps),
        (jax.ShapeDtypeStruct((tile, steps * width), BF16),) * 2,
        [sm] + [any_] * (1 + cols_count),
        [wide, wide, dma((steps * (cols_count + 1),))],
        "ordered",
        20,
        5,
    )(scal, probe, *ar)
    gathered = []
    for k in range(steps):
        x = jnp.concatenate(blocks, 1)
        x = after(x, *gathered[k - 1][3:]) if k > 0 else after(x, core, al[-1])
        x1 = exchange(x, "row", rows_count, one)
        x2 = exchange(x, "row", rows_count, two)
        before = ()
        if k == 0:
            blocks, _ = own_blocks(1, x)
            before = (cross, *ordered)
        l3 = exchange(after(x1[0], *before), "row", rows_count, two)
        r3 = exchange(after(x2[1], *before), "row", rows_count, one)
        gathered.append((x, x1, x2, l3, r3))

    mid0, rp01, k0, y0, gram = call(
        functools.partial(first_kernel, steps),
        (f32(width, width), f32(width, width), f32(2 * width, width), f32(2 * width, width), f32(width, width)),
        [sm] + [vm] * 9,
        [],
        "first_step",
        20,
        20,
    )(scal, *ordered, *gathered[0], core, cross)
    w0, core_c, h0 = call(
        functools.partial(inverse_kernel, tile),
        (f32(width, width),) * 3,
        [sm] + [vm] * 7,
        [VMEM((width, 2 * width), F32)],
        "inverse_factor",
        24,
        30,
    )(scal, gram, k0, y0, cross, mid0, rp01, core)
    weights = VMEM(((3 + 2 * steps) * width, width), BF16)
    late_b = [g[i] for g in (gathered[1], gathered[0]) for i in (0, 1, 2, 4)]
    out_left, out_right = call(
        functools.partial(second_kernel, masks_a, masks_b, steps),
        (f32(tile, width), f32(tile, width)),
        [sm] + [vm] * 14 + [any_] * (10 + cols_count),
        [
            whole, whole, wide, wide, VMEM((width, width), F32), weights, weights, whole, whole,
            dma((2 * rows_count + steps * cols_count + 2,)), dma((2 * (tile // CHUNK),)),
        ],
        "second_step",
        36,
        100,
        ANY,
    )(scal, k0, y0, w0, core_c, h0, mid0, cross, *ordered, *gathered[1], left, right, *late_b, *al)
    return (out_left[None, None], out_right[None, None])


def solution(mesh):
    return jax.shard_map(
        functools.partial(on_device, mesh.shape["row"], mesh.shape["col"]),
        mesh=mesh,
        in_specs=(
            P("row", "col", None, None),
            P("row", "col", None, None),
            P("row", "col"),
            P("row", None, "col", None),
            P("row", None, "col", None),
            P("row", None),
            P("row", None),
            P(None, "col", "row", None),
            P(None, "col", "row", None),
            P(None, "col"),
            P(None, "col"),
            P(),
            P("row", "col", None),
        ),
        out_specs=(P("row", "col", None, None), P("row", "col", None, None)),
        check_vma=False,
    )
```

```python
import functools
import math

import jax
import jax.numpy as jnp
from jax import lax
from jax.experimental import pallas as pl
from jax.experimental.pallas import tpu as pltpu
from jax.sharding import PartitionSpec as P

F32 = jnp.float32
BF16 = jnp.bfloat16
ANY = pl.ANY
VMEM = pltpu.VMEM
SMEM = pltpu.SMEM
PANEL = 64
CHUNK = 256


def exchange(x, axis, size, bit):
    return lax.ppermute(x, axis, [(r, r ^ bit) for r in range(size)])


def spread(x, axis, size, bits):
    masks = [0]
    for bit in bits:
        masks += [mask ^ bit for mask in masks]
    masks = sorted(masks, reverse=True)[:-1]
    return [x] + [exchange(x, axis, size, mask) for mask in masks], [0] + masks


def forwarded(x, axis, size, bits):
    blocks, masks = [x], [0]
    for bit in bits:
        blocks += [exchange(block, axis, size, bit) for block in blocks]
        masks += [mask ^ bit for mask in masks]
    return blocks, masks


def after(x, *before):
    return lax.optimization_barrier((x, *before))[0]


def bits_of(size):
    bits = []
    bit = size // 2
    while bit >= 1:
        bits.append(bit)
        bit //= 2
    return bits


def split2(x):
    high = x.astype(BF16)
    return high, (x - high.astype(F32)).astype(BF16)


def mm(a, b):
    return lax.dot_general(a, b, (((1,), (0,)), ((), ())), preferred_element_type=F32)


def mm_at(a, b):
    return lax.dot_general(a, b, (((0,), (0,)), ((), ())), preferred_element_type=F32)


def mm_bt(a, b):
    return lax.dot_general(a, b, (((1,), (1,)), ((), ())), preferred_element_type=F32)


def close(a, b):
    a_h, a_m = split2(a)
    b_h, b_m = split2(b)
    return mm(jnp.concatenate([a_h, a_m, a_h], 1), jnp.concatenate([b_h, b_h, b_m], 0))


def close_at(a, b):
    a_h, a_m = split2(a)
    b_h, b_m = split2(b)
    return mm_at(jnp.concatenate([a_h, a_m, a_h], 0), jnp.concatenate([b_h, b_h, b_m], 0))


def close_bt(a, b):
    a_h, a_m = split2(a)
    b_h, b_m = split2(b)
    return mm_bt(jnp.concatenate([a_h, a_m, a_h], 1), jnp.concatenate([b_h, b_h, b_m], 1))


def exact(a, b):
    return lax.dot_general(
        a, b, (((1,), (0,)), ((), ())), precision=lax.Precision.HIGHEST, preferred_element_type=F32
    )


def exact_at(a, b):
    return lax.dot_general(
        a, b, (((0,), (0,)), ((), ())), precision=lax.Precision.HIGHEST, preferred_element_type=F32
    )


def split3(x):
    high, mid = split2(x)
    return high, mid, (x - high.astype(F32) - mid.astype(F32)).astype(BF16)


def stacked_at(a, b):
    a_h, a_m, a_l = split3(a)
    b_h, b_m, b_l = split3(b)
    return mm_at(jnp.concatenate([a_h, a_h, a_m, a_m, a_h, a_l], 0), jnp.concatenate([b_h, b_m, b_h, b_m, b_l, b_h], 0))


def lanes_below(count, rows, width):
    return (lax.broadcasted_iota(jnp.int32, (rows, width), 1) < count).astype(F32)


def rows_below(count, rows, width):
    return (lax.broadcasted_iota(jnp.int32, (rows, width), 0) < count).astype(F32)


def place(srcs, masks, index, dst, sems, first):
    copies = []
    for src, owners in zip(srcs, masks):
        for at, mask in enumerate(owners):
            block = src.at[at]
            rows = block.shape[0]
            start = pl.multiple_of((index ^ mask) * rows, 16)
            copies.append(
                pltpu.make_async_copy(block, dst.at[pl.ds(start, rows), :], sems.at[first + len(copies)])
            )
    return copies


def lane_of(x, at):
    return jnp.broadcast_to(x[:, at : at + 1], (8, 128))


def row_of(x, at):
    return jnp.broadcast_to(x[at : at + 1, :], (8, x.shape[1]))


def factor_panel(rows, first, width, between):
    count = len(rows)
    lane = lax.broadcasted_iota(jnp.int32, (8, width), 1)
    sub_wide = lax.broadcasted_iota(jnp.int32, (8, width), 0)
    sub = lax.broadcasted_iota(jnp.int32, (8, 128), 0)
    wide = lambda x: jnp.concatenate([x] * (width // 128), 1)
    for s in range(count):
        c0 = first + 8 * s
        col = {}
        for l in range(8):
            for q in range(s, count):
                col[l, q] = lane_of(rows[q], c0 + l)
        inside = (lane >= c0) & (lane < c0 + 8)
        unit = jnp.where(lane == c0 + sub_wide, 1.0, 0.0)
        for q in range(s, count):
            rows[q] = jnp.where(inside, unit if q == s else 0.0, rows[q])
        pivots = jnp.ones((8, 128), F32)
        for l in range(8):
            d = row_of(col[l, s], l)
            inverse = 1.0 / d
            pivots = jnp.where(sub == l, d, pivots)
            mult = {}
            for q in range(s, count):
                mult[q] = col[l, q] * inverse
                if q == s:
                    mult[q] = jnp.where(sub > l, mult[q], 0.0)
            for l2 in range(l + 1, 8):
                e = row_of(col[l, s], l2)
                for q in range(s, count):
                    col[l2, q] = col[l2, q] - mult[q] * e
            pivot_row = row_of(rows[s], l)
            for q in range(s, count):
                rows[q] = rows[q] - wide(mult[q]) * pivot_row
        rows[s] = rows[s] * wide(lax.rsqrt(pivots))
        between(c0 // 8)
    return rows


def inverse_factor(work, beside=(), start=0, stop=None):
    n = work.shape[0]
    beside = list(beside)
    slots = n // PANEL
    stop = slots if stop is None else stop
    for p in range(start, stop):
        a = p * PANEL
        b = a + PANEL
        rows = [work[a + 8 * i : a + 8 * i + 8, :] for i in range(PANEL // 8)]
        rows = factor_panel(rows, a, n, functools.partial(some_of, beside, stop * PANEL // 8))
        for i in range(PANEL // 8):
            work[a + 8 * i : a + 8 * i + 8, :] = rows[i]
        if b < n:
            full = jnp.concatenate(rows, 0)
            lane = lax.broadcasted_iota(jnp.int32, (PANEL, n), 1)
            row = lax.broadcasted_iota(jnp.int32, (PANEL, n), 0)
            kept = jnp.where((lane > a + row) & (lane < b), 0.0, full)
            base = b // 128 * 128
            update = stacked_at(full[:, base:], kept)[b - base :]
            lane = lax.broadcasted_iota(jnp.int32, (n - b, n), 1)
            rest = jnp.where((lane >= a) & (lane < b), 0.0, work[b:, :])
            work[b:, :] = rest - update
    while beside:
        beside.pop(0)()
    if stop < slots:
        return
    row = lax.broadcasted_iota(jnp.int32, (n, n), 0)
    lane = lax.broadcasted_iota(jnp.int32, (n, n), 1)
    work[...] = jnp.where(lane <= row, work[...], 0.0)


def some_of(beside, slabs, slab):
    for _ in range(-(-len(beside) // (slabs - slab))):
        beside.pop(0)()


def unit_beyond(count, width):
    row = lax.broadcasted_iota(jnp.int32, (width, width), 0)
    lane = lax.broadcasted_iota(jnp.int32, (width, width), 1)
    return jnp.where((row == lane) & (row >= count), 1.0, 0.0)


def probe_kernel(steps, right, probe, out, right_v, probe_v, sems):
    tile, width = right_v.shape
    copies = [pltpu.make_async_copy(right, right_v, sems.at[0])]
    for k in range(steps):
        here = probe_v.at[:, pl.ds(k * width, width)]
        copies.append(pltpu.make_async_copy(probe.at[k], here, sems.at[1 + k]))
    for copy in copies:
        copy.start()
    for copy in copies:
        copy.wait()
    high, mid = split2(right_v[...])
    both = probe_v[...]
    total = mm_at(high, both) + mm_at(mid, both)
    for k in range(steps):
        out[k] = total[:, k * width : (k + 1) * width]


def cross_kernel(masks_a, steps, scal, left, *refs):
    al, (out, left_v, parts_v, sems) = refs[: len(masks_a)], refs[len(masks_a) :]
    tile, width = left_v.shape
    copy_left = pltpu.make_async_copy(left, left_v, sems.at[0])
    copies = []
    for k in range(steps):
        here = parts_v.at[:, pl.ds((2 + k) * width, width)]
        copies += place([r.at[:, k] for r in al], masks_a, scal[1 + 4 * steps], here, sems, 1 + len(copies))
    copy_left.start()
    for copy in copies:
        copy.start()
    copy_left.wait()
    high, mid = split2(left_v[...])
    parts_v[:, :width] = high
    parts_v[:, width : 2 * width] = mid
    for copy in copies:
        copy.wait()
    x = mm_at(parts_v[:, :width], parts_v[...])
    y = mm_at(parts_v[:, width : 2 * width], parts_v[:, width:])
    hm = x[:, width : 2 * width]
    out[:width, :width] = x[:, :width] + hm + hm.T + y[:, :width]
    la = x[:, 2 * width :] + y[:, width:]
    out[:width, width:] = la
    out[width:, :width] = la.T
    out[width:, width:] = mm_at(parts_v[:, 2 * width :], parts_v[:, 2 * width :])


def order_kernel(masks_a, masks_b, steps, scal, probe, *refs):
    ar, (ar_out, probe_out, ar_v, probe_v, sems) = refs[: len(masks_a)], refs[len(masks_a) :]
    col_at, row_at = scal[1 + 4 * steps], scal[2 + 4 * steps]
    copies = []
    for k in range(steps):
        here = pl.ds(k * ar_v.shape[1] // steps, ar_v.shape[1] // steps)
        copies += place([r.at[:, k] for r in ar], masks_a, col_at, ar_v.at[:, here], sems, len(copies))
        copies.append(pltpu.make_async_copy(probe.at[k], probe_v.at[:, here], sems.at[len(copies)]))
    for copy in copies:
        copy.start()
    for copy in copies:
        copy.wait()
    masks = sum(masks_b, [])
    rows = ar_v.shape[0] // len(masks)
    for at, mask in enumerate(masks):
        start = pl.multiple_of((row_at ^ mask) * rows, 16)
        ar_out[at * rows : (at + 1) * rows, :] = ar_v[pl.ds(start, rows), :]
        probe_out[at * rows : (at + 1) * rows, :] = probe_v[pl.ds(start, rows), :]


def summed(lefts, rights):
    total = None
    for left, right in zip(lefts, rights):
        part = mm_at(left, right)
        total = part if total is None else total + part
    return total


def pieces_of(refs):
    return [r[...].reshape(r.shape[0] * r.shape[1], r.shape[2]) for r in refs]


def split_rows(ref, count, at, width):
    rows = ref.shape[0] // count
    return [ref[i * rows : (i + 1) * rows, at : at + width] for i in range(count)]


def masked(scal, step, steps, mid):
    width = mid.shape[0]
    weight = scal[1 + 3 * steps + step].astype(F32)
    a_rank, b_rank = scal[1 + steps + step], scal[1 + 2 * steps + step]
    return mid * rows_below(a_rank, width, width) * lanes_below(b_rank, width, width) * weight


def first_kernel(steps, scal, ar, probe, *refs):
    (x, x1, x2, l3, r3), (core, cross, mid_out, rp_out, k_out, y_out, gram_out) = refs[:5], refs[5:]
    width = mid_out.shape[0]
    tmask = lanes_below(scal[1], width, width)
    k_out[:width, :] = core[0] * rows_below(scal[0], width, width) * tmask
    b_left, b_right = pieces_of([x.at[0], x1.at[0], x2.at[0], l3]), pieces_of([x.at[1], x1.at[1], x2.at[1], r3])
    mid = masked(scal, 0, steps, summed(split_rows(ar, 4, 0, width), b_left))
    mid_out[...] = mid
    rp = summed(b_right, split_rows(probe, 4, 0, steps * width))
    rp_out[...] = rp[:, width:]
    k_out[width:, :] = exact(mid, rp[:, :width] * tmask)
    k = k_out[...]
    y = exact(cross[: 2 * width, : 2 * width], k)
    y_out[...] = y
    gram_out[...] = exact_at(k, y) + unit_beyond(scal[1], width)


def early_kernel(tile, scal, gram, k0, y0, cross, mid0, rp01, core, work_out, t_out):
    width = gram.shape[0]
    root = math.sqrt(tile)
    work_out[...] = gram[...]

    def next_core():
        y = jnp.concatenate([y0[:width, :] * rows_below(scal[0], width, width), y0[width:, :]], 0)
        z = jnp.concatenate([core[1], exact(mid0[...], rp01[...])], 0)
        t_out[:, :width] = exact_at(y, z) * (1.0 / root)

    def next_cross():
        t_out[:, width:] = exact(cross[2 * width :, : 2 * width], k0[...]).T * root

    inverse_factor(work_out, [next_core, next_cross], 0, width // PANEL // 2)


def late_kernel(masks_a, steps, scal, work, t, k0, y0, mid0, ar, probe, x, x1, x2, left, *refs):
    n = len(masks_a)
    al, (core_out, h_out, h_a_out, mid_out, rp_out, k_out, back_out, s_out) = refs[:n], refs[n : n + 8]
    work_v, left_v, a_v, sems = refs[n + 8 :]
    tile, width = left_v.shape
    root = math.sqrt(tile)
    late = place([r.at[:, 0] for r in al], masks_a, scal[1 + 4 * steps], a_v, sems, 0)
    late.append(pltpu.make_async_copy(left, left_v, sems.at[n]))
    work_v[...] = work[...]

    def fetch():
        for copy in late:
            copy.start()

    def middle_part():
        mid_out[...] = summed(split_rows(ar, 4, width, width)[:3], pieces_of([r.at[0] for r in (x, x1, x2)]))

    def probe_part():
        rp_out[...] = summed(pieces_of([r.at[1] for r in (x, x1, x2)]), split_rows(probe, 4, width, width)[:3])

    inverse_factor(work_v, [fetch, middle_part, probe_part], width // PANEL // 2)
    w = work_v[...]
    both = exact(w, t[...])
    keep = rows_below(scal[1], width, width)
    a = both[:, :width] * keep * lanes_below(scal[2], width, width)
    h = both[:, width:] * keep
    core_out[...] = a
    h_out[...] = h
    h_a_out[...] = exact_at(h, a)
    k_c = close(k0[...], close_at(w, a) * root)
    k_out[...] = k_c
    z = close_bt(y0[...], w)
    back_out[:width, :] = z[:width] * rows_below(scal[0], width, width)
    back_out[width:, :] = close_at(mid0[...], z[width:])
    k_h, k_m = split2(k_c)
    weights = jnp.concatenate([k_h[:width], k_h[:width], k_m[:width], k_h[width:], k_m[width:]], 0)
    for copy in late:
        copy.wait()
    for c in range(tile // CHUNK):
        at = slice(c * CHUNK, (c + 1) * CHUNK)
        l_h, l_m = split2(left_v[at, :])
        o = a_v[at, :]
        s_out[at, :] = mm(jnp.concatenate([l_h, l_m, l_h, o, o], 1), weights)


def second_kernel(
    masks_a, masks_b, steps, scal, core_c, h0, h_a, mid_part, rp_part, k_c, back0, s_part, cross, ar, probe,
    l3, r3, right, b0, b1, b2, br3, p0, p1, p2, pr3, *refs,
):
    n = len(masks_a)
    al, (out_left, out_right), refs = refs[:n], refs[n : n + 2], refs[n + 2 :]
    right_v, a_v, b_v, gram_v, k_v, q_v, outl_v, outr_v, sems, out_sems = refs
    tile, width = right_v.shape
    root = math.sqrt(tile)
    col_at, row_at = scal[1 + 4 * steps], scal[2 + 4 * steps]
    late = place([r.at[:, 1] for r in al], masks_a, col_at, a_v, sems, 0)
    for k, (x, x1, x2, x3) in enumerate(((p0, p1, p2, pr3), (b0, b1, b2, br3))):
        here = pl.ds(k * width, width)
        late += place((x.at[1], x1.at[1], x2.at[1], x3), masks_b, row_at, b_v.at[:, here], sems, len(late))
    late.append(pltpu.make_async_copy(right, right_v, sems.at[len(late)]))
    t0, t1 = scal[1], scal[2]
    a = core_c[...]
    h = h0[...]
    mid1 = masked(scal, 1, steps, mid_part[...] + summed(split_rows(ar, 4, width, width)[3:], pieces_of([l3])))
    rp11 = rp_part[...] + summed(pieces_of([r3]), split_rows(probe, 4, width, width)[3:])
    core_b = exact(mid1, rp11 * lanes_below(t1, width, width))
    both = exact(jnp.concatenate([h, cross[2 * width :, 2 * width :]], 0), core_b)
    top = a * float(tile) + both[:width]
    low = h_a[...] + both[width:]
    gram_v[...] = exact_at(jnp.concatenate([a, core_b], 0), jnp.concatenate([top, low], 0)) + unit_beyond(t1, width)

    def left_weights():
        k_v[...] = jnp.concatenate(split2(core_b), 0)

    def right_weights():
        q_c = close(back0[...], top * rows_below(t0, width, width)) * (1.0 / tile)
        h, m = split2(jnp.concatenate([q_c, close_at(mid1, low) * (1.0 / root)], 0))
        q_v[...] = jnp.concatenate([h[:width], h[:width], m[:width], h[width:], m[width:]], 0)

    def fetch():
        for copy in late:
            copy.start()

    def arrive():
        for copy in late:
            copy.wait()

    def form_left(c):
        at = slice(c * CHUNK, (c + 1) * CHUNK)
        o = a_v[at, :]
        outl_v[at, :] = s_part[at, :] + mm(jnp.concatenate([o, o], 1), k_v[...])

    def form_right(c):
        at = slice(c * CHUNK, (c + 1) * CHUNK)
        h, m = split2(right_v[at, :])
        o = b_v[at, :]
        outr_v[at, :] = mm(jnp.concatenate([h, m, h, o, o], 1), q_v[...])

    count = tile // CHUNK
    beside = [fetch, left_weights, right_weights, arrive]
    for form in (form_left, form_right):
        beside += [functools.partial(form, c) for c in range(count)]
    inverse_factor(gram_v, beside)
    h, m = split2(gram_v[...])
    weights = jnp.concatenate([h, h, m], 1)
    outs = []
    for c in range(count):
        at = pl.ds(c * CHUNK, CHUNK)
        for src, dst, scale in ((outl_v, out_left, root), (outr_v, out_right, 1.0)):
            h, m = split2(src[at, :])
            src[at, :] = mm_bt(jnp.concatenate([h, m, h], 1), weights) * scale
            copy = pltpu.make_async_copy(src.at[at, :], dst.at[at, :], out_sems.at[len(outs)])
            copy.start()
            outs.append(copy)
    for copy in outs:
        copy.wait()


def call(kernel, out_shape, in_specs, scratch, name, vmem, passes, out_space=VMEM):
    flops = passes * 2 * 2048 * 256 * 256
    return pl.pallas_call(
        kernel,
        out_shape=out_shape,
        in_specs=in_specs,
        out_specs=jax.tree.map(lambda _: pl.BlockSpec(memory_space=out_space), out_shape),
        scratch_shapes=scratch,
        compiler_params=pltpu.CompilerParams(vmem_limit_bytes=vmem * 1024 * 1024),
        cost_estimate=pl.CostEstimate(flops=flops, bytes_accessed=1 << 20, transcendentals=0),
        name=name,
    )


def on_device(
    rows_count, cols_count, c_left, c_right, c_rank, a_left, a_right, a_rank, a_pattern,
    b_left, b_right, b_rank, b_pattern, probe, target,
):
    tile, width = c_left.shape[2:]
    steps = probe.shape[0]
    left = c_left[0, 0]
    right = c_right[0, 0]
    any_, vm, sm = (pl.BlockSpec(memory_space=s) for s in (ANY, VMEM, SMEM))
    dma = pltpu.SemaphoreType.DMA

    def f32(*shape):
        return jax.ShapeDtypeStruct(shape, F32)

    scal = jnp.concatenate(
        [
            c_rank[0],
            target[0, 0],
            a_rank[0],
            b_rank[:, 0],
            a_pattern[0] * b_pattern[:, 0],
            jnp.stack([lax.axis_index("col"), lax.axis_index("row")]),
        ]
    ).astype(jnp.int32)

    whole = VMEM((tile, width), F32)
    wide = VMEM((tile, steps * width), BF16)
    a_bits = bits_of(cols_count)
    al, masks = spread(a_left, "col", cols_count, a_bits)
    ar, _ = spread(a_right, "col", cols_count, a_bits)
    masks_a = [[mask] for mask in masks]
    bits = bits_of(rows_count)
    one, two = bits[-1], bits[-2]
    core = call(
        functools.partial(probe_kernel, steps),
        f32(steps, width, width),
        [any_, any_],
        [VMEM((tile, width), F32), VMEM((tile, steps * width), BF16), dma((1 + steps,))],
        "right_probe",
        16,
        12,
    )(right, probe)
    cross = call(
        functools.partial(cross_kernel, masks_a, steps),
        f32((1 + steps) * width, (1 + steps) * width),
        [sm] + [any_] * (1 + cols_count),
        [VMEM((tile, width), F32), VMEM((tile, (2 + steps) * width), BF16), dma((1 + steps * cols_count,))],
        "left_cross",
        24,
        24,
    )(scal, left, *al)

    def own_blocks(k, *before):
        x = jnp.stack([b_left[k, 0], b_right[k, 0]])[:, None]
        return (forwarded if True else spread)(after(x, *before) if before else x, "row", rows_count, bits[:-2])

    blocks, masks = own_blocks(0)
    masks_b = [[mask ^ flip for mask in masks] for flip in (0, one, two, one ^ two)]
    ordered = call(
        functools.partial(order_kernel, masks_a, masks_b, steps),
        (jax.ShapeDtypeStruct((tile, steps * width), BF16),) * 2,
        [sm] + [any_] * (1 + cols_count),
        [wide, wide, dma((steps * (cols_count + 1),))],
        "ordered",
        20,
        5,
    )(scal, probe, *ar)
    gathered = []
    for k in range(steps):
        x = jnp.concatenate(blocks, 1)
        x = after(x, *gathered[k - 1][3:]) if k > 0 else after(x, core, al[-1])
        x1 = exchange(x, "row", rows_count, one)
        x2 = exchange(x, "row", rows_count, two)
        before = ()
        if k == 0:
            blocks, _ = own_blocks(1, x)
            before = (cross, *ordered)
        l3 = exchange(after(x1[0], *before), "row", rows_count, two)
        r3 = exchange(after(x2[1], *before), "row", rows_count, one)
        gathered.append((x, x1, x2, l3, r3))

    mid0, rp01, k0, y0, gram = call(
        functools.partial(first_kernel, steps),
        (f32(width, width), f32(width, width), f32(2 * width, width), f32(2 * width, width), f32(width, width)),
        [sm] + [vm] * 9,
        [],
        "first_step",
        20,
        20,
    )(scal, *ordered, *gathered[0], core, cross)
    square = f32(width, width)
    work, t = call(
        functools.partial(early_kernel, tile),
        (square, f32(width, 2 * width)),
        [sm] + [vm] * 7,
        [],
        "factor_early",
        20,
        15,
    )(scal, gram, k0, y0, cross, mid0, rp01, core)
    x, x1, x2, l3, r3 = gathered[1]
    tall = f32(2 * width, width)
    state = call(
        functools.partial(late_kernel, masks_a, steps),
        (square, square, square, square, square, tall, tall, f32(tile, width)),
        [sm] + [vm] * 10 + [any_] * (1 + cols_count),
        [VMEM((width, width), F32), whole, VMEM((tile, width), BF16), dma((cols_count + 1,))],
        "factor_late",
        24,
        25,
    )(scal, work, t, k0, y0, mid0, *ordered, x, x1, x2, left, *al)
    out_left, out_right = call(
        functools.partial(second_kernel, masks_a, masks_b, steps),
        (f32(tile, width), f32(tile, width)),
        [sm] + [vm] * 13 + [any_] * (9 + cols_count),
        [
            whole, VMEM((tile, width), BF16), wide, VMEM((width, width), F32),
            VMEM((2 * width, width), BF16), VMEM(((3 + 2 * steps) * width, width), BF16), whole, whole,
            dma((2 * rows_count + cols_count + 1,)), dma((2 * (tile // CHUNK),)),
        ],
        "second_step",
        36,
        100,
        ANY,
    )(
        scal, *state, cross, *ordered, l3, r3, right, x, x1, x2, r3, *[gathered[0][i] for i in (0, 1, 2, 4)], *al
    )
    return (out_left[None, None], out_right[None, None])


def solution(mesh):
    return jax.shard_map(
        functools.partial(on_device, mesh.shape["row"], mesh.shape["col"]),
        mesh=mesh,
        in_specs=(
            P("row", "col", None, None),
            P("row", "col", None, None),
            P("row", "col"),
            P("row", None, "col", None),
            P("row", None, "col", None),
            P("row", None),
            P("row", None),
            P(None, "col", "row", None),
            P(None, "col", "row", None),
            P(None, "col"),
            P(None, "col"),
            P(),
            P("row", "col", None),
        ),
        out_specs=(P("row", "col", None, None), P("row", "col", None, None)),
        check_vma=False,
    )
```

```python
import functools
import math

import jax
import jax.numpy as jnp
from jax import lax
from jax.experimental import pallas as pl
from jax.experimental.pallas import tpu as pltpu
from jax.sharding import PartitionSpec as P

F32 = jnp.float32
BF16 = jnp.bfloat16
ANY = pl.ANY
VMEM = pltpu.VMEM
SMEM = pltpu.SMEM
PANEL = 32
CHUNK = 256


def exchange(x, axis, size, bit):
    return lax.ppermute(x, axis, [(r, r ^ bit) for r in range(size)])


def spread(x, axis, size, bits):
    masks = [0]
    for bit in bits:
        masks += [mask ^ bit for mask in masks]
    masks = sorted(masks, reverse=True)[:-1]
    return [x] + [exchange(x, axis, size, mask) for mask in masks], [0] + masks


def forwarded(x, axis, size, bits):
    blocks, masks = [x], [0]
    for bit in bits:
        blocks += [exchange(block, axis, size, bit) for block in blocks]
        masks += [mask ^ bit for mask in masks]
    return blocks, masks


def after(x, *before):
    return lax.optimization_barrier((x, *before))[0]


def bits_of(size):
    bits = []
    bit = size // 2
    while bit >= 1:
        bits.append(bit)
        bit //= 2
    return bits


def split2(x):
    high = x.astype(BF16)
    return high, (x - high.astype(F32)).astype(BF16)


def mm(a, b):
    return lax.dot_general(a, b, (((1,), (0,)), ((), ())), preferred_element_type=F32)


def mm_at(a, b):
    return lax.dot_general(a, b, (((0,), (0,)), ((), ())), preferred_element_type=F32)


def mm_bt(a, b):
    return lax.dot_general(a, b, (((1,), (1,)), ((), ())), preferred_element_type=F32)


def close(a, b):
    a_h, a_m = split2(a)
    b_h, b_m = split2(b)
    return mm(jnp.concatenate([a_h, a_m, a_h], 1), jnp.concatenate([b_h, b_h, b_m], 0))


def close_at(a, b):
    a_h, a_m = split2(a)
    b_h, b_m = split2(b)
    return mm_at(jnp.concatenate([a_h, a_m, a_h], 0), jnp.concatenate([b_h, b_h, b_m], 0))


def close_bt(a, b):
    a_h, a_m = split2(a)
    b_h, b_m = split2(b)
    return mm_bt(jnp.concatenate([a_h, a_m, a_h], 1), jnp.concatenate([b_h, b_h, b_m], 1))


def exact(a, b):
    return lax.dot_general(
        a, b, (((1,), (0,)), ((), ())), precision=lax.Precision.HIGHEST, preferred_element_type=F32
    )


def exact_at(a, b):
    return lax.dot_general(
        a, b, (((0,), (0,)), ((), ())), precision=lax.Precision.HIGHEST, preferred_element_type=F32
    )


def split3(x):
    high, mid = split2(x)
    return high, mid, (x - high.astype(F32) - mid.astype(F32)).astype(BF16)


def stacked_at(a, b):
    a_h, a_m, a_l = split3(a)
    b_h, b_m, b_l = split3(b)
    return mm_at(jnp.concatenate([a_h, a_h, a_m, a_m, a_h, a_l], 0), jnp.concatenate([b_h, b_m, b_h, b_m, b_l, b_h], 0))


def lanes_below(count, rows, width):
    return (lax.broadcasted_iota(jnp.int32, (rows, width), 1) < count).astype(F32)


def rows_below(count, rows, width):
    return (lax.broadcasted_iota(jnp.int32, (rows, width), 0) < count).astype(F32)


def place(srcs, masks, index, dst, sems, first):
    copies = []
    for src, owners in zip(srcs, masks):
        for at, mask in enumerate(owners):
            block = src.at[at]
            rows = block.shape[0]
            start = pl.multiple_of((index ^ mask) * rows, 16)
            copies.append(
                pltpu.make_async_copy(block, dst.at[pl.ds(start, rows), :], sems.at[first + len(copies)])
            )
    return copies


def lane_of(x, at):
    return jnp.broadcast_to(x[:, at : at + 1], (8, 128))


def row_of(x, at):
    return jnp.broadcast_to(x[at : at + 1, :], (8, x.shape[1]))


def factor_panel(rows, first, width, between):
    count = len(rows)
    lane = lax.broadcasted_iota(jnp.int32, (8, width), 1)
    sub_wide = lax.broadcasted_iota(jnp.int32, (8, width), 0)
    sub = lax.broadcasted_iota(jnp.int32, (8, 128), 0)
    wide = lambda x: jnp.concatenate([x] * (width // 128), 1)
    for s in range(count):
        c0 = first + 8 * s
        col = {}
        for l in range(8):
            for q in range(s, count):
                col[l, q] = lane_of(rows[q], c0 + l)
        inside = (lane >= c0) & (lane < c0 + 8)
        unit = jnp.where(lane == c0 + sub_wide, 1.0, 0.0)
        for q in range(s, count):
            rows[q] = jnp.where(inside, unit if q == s else 0.0, rows[q])
        pivots = jnp.ones((8, 128), F32)
        for l in range(8):
            d = row_of(col[l, s], l)
            inverse = 1.0 / d
            pivots = jnp.where(sub == l, d, pivots)
            mult = {}
            for q in range(s, count):
                mult[q] = col[l, q] * inverse
                if q == s:
                    mult[q] = jnp.where(sub > l, mult[q], 0.0)
            for l2 in range(l + 1, 8):
                e = row_of(col[l, s], l2)
                for q in range(s, count):
                    col[l2, q] = col[l2, q] - mult[q] * e
            pivot_row = row_of(rows[s], l)
            for q in range(s, count):
                rows[q] = rows[q] - wide(mult[q]) * pivot_row
        rows[s] = rows[s] * wide(lax.rsqrt(pivots))
        between(c0 // 8)
    return rows


def inverse_factor(work, beside=(), start=0, stop=None):
    n = work.shape[0]
    beside = list(beside)
    slots = n // PANEL
    stop = slots if stop is None else stop
    for p in range(start, stop):
        a = p * PANEL
        b = a + PANEL
        rows = [work[a + 8 * i : a + 8 * i + 8, :] for i in range(PANEL // 8)]
        rows = factor_panel(rows, a, n, functools.partial(some_of, beside, stop * PANEL // 8))
        for i in range(PANEL // 8):
            work[a + 8 * i : a + 8 * i + 8, :] = rows[i]
        if b < n:
            full = jnp.concatenate(rows, 0)
            lane = lax.broadcasted_iota(jnp.int32, (PANEL, n), 1)
            row = lax.broadcasted_iota(jnp.int32, (PANEL, n), 0)
            kept = jnp.where((lane > a + row) & (lane < b), 0.0, full)
            base = b // 128 * 128
            update = stacked_at(full[:, base:], kept)[b - base :]
            lane = lax.broadcasted_iota(jnp.int32, (n - b, n), 1)
            rest = jnp.where((lane >= a) & (lane < b), 0.0, work[b:, :])
            work[b:, :] = rest - update
    while beside:
        beside.pop(0)()
    if stop < slots:
        return
    row = lax.broadcasted_iota(jnp.int32, (n, n), 0)
    lane = lax.broadcasted_iota(jnp.int32, (n, n), 1)
    work[...] = jnp.where(lane <= row, work[...], 0.0)


def some_of(beside, slabs, slab):
    for _ in range(-(-len(beside) // (slabs - slab))):
        beside.pop(0)()


def unit_beyond(count, width):
    row = lax.broadcasted_iota(jnp.int32, (width, width), 0)
    lane = lax.broadcasted_iota(jnp.int32, (width, width), 1)
    return jnp.where((row == lane) & (row >= count), 1.0, 0.0)


def probe_kernel(steps, right, probe, out, right_v, probe_v, sems):
    tile, width = right_v.shape
    copies = [pltpu.make_async_copy(right, right_v, sems.at[0])]
    for k in range(steps):
        here = probe_v.at[:, pl.ds(k * width, width)]
        copies.append(pltpu.make_async_copy(probe.at[k], here, sems.at[1 + k]))
    for copy in copies:
        copy.start()
    for copy in copies:
        copy.wait()
    high, mid = split2(right_v[...])
    both = probe_v[...]
    total = mm_at(high, both) + mm_at(mid, both)
    for k in range(steps):
        out[k] = total[:, k * width : (k + 1) * width]


def cross_kernel(masks_a, steps, scal, left, *refs):
    al, (out, left_v, parts_v, sems) = refs[: len(masks_a)], refs[len(masks_a) :]
    tile, width = left_v.shape
    copy_left = pltpu.make_async_copy(left, left_v, sems.at[0])
    copies = []
    for k in range(steps):
        here = parts_v.at[:, pl.ds((2 + k) * width, width)]
        copies += place([r.at[:, k] for r in al], masks_a, scal[1 + 4 * steps], here, sems, 1 + len(copies))
    copy_left.start()
    for copy in copies:
        copy.start()
    copy_left.wait()
    high, mid = split2(left_v[...])
    parts_v[:, :width] = high
    parts_v[:, width : 2 * width] = mid
    for copy in copies:
        copy.wait()
    x = mm_at(parts_v[:, :width], parts_v[...])
    y = mm_at(parts_v[:, width : 2 * width], parts_v[:, width:])
    hm = x[:, width : 2 * width]
    out[:width, :width] = x[:, :width] + hm + hm.T + y[:, :width]
    la = x[:, 2 * width :] + y[:, width:]
    out[:width, width:] = la
    out[width:, :width] = la.T
    out[width:, width:] = mm_at(parts_v[:, 2 * width :], parts_v[:, 2 * width :])


def order_kernel(masks_a, masks_b, steps, scal, probe, *refs):
    ar, (ar_out, probe_out, ar_v, probe_v, sems) = refs[: len(masks_a)], refs[len(masks_a) :]
    col_at, row_at = scal[1 + 4 * steps], scal[2 + 4 * steps]
    copies = []
    for k in range(steps):
        here = pl.ds(k * ar_v.shape[1] // steps, ar_v.shape[1] // steps)
        copies += place([r.at[:, k] for r in ar], masks_a, col_at, ar_v.at[:, here], sems, len(copies))
        copies.append(pltpu.make_async_copy(probe.at[k], probe_v.at[:, here], sems.at[len(copies)]))
    for copy in copies:
        copy.start()
    for copy in copies:
        copy.wait()
    masks = sum(masks_b, [])
    rows = ar_v.shape[0] // len(masks)
    for at, mask in enumerate(masks):
        start = pl.multiple_of((row_at ^ mask) * rows, 16)
        ar_out[at * rows : (at + 1) * rows, :] = ar_v[pl.ds(start, rows), :]
        probe_out[at * rows : (at + 1) * rows, :] = probe_v[pl.ds(start, rows), :]


def summed(lefts, rights):
    total = None
    for left, right in zip(lefts, rights):
        part = mm_at(left, right)
        total = part if total is None else total + part
    return total


def pieces_of(refs):
    return [r[...].reshape(r.shape[0] * r.shape[1], r.shape[2]) for r in refs]


def split_rows(ref, count, at, width):
    rows = ref.shape[0] // count
    return [ref[i * rows : (i + 1) * rows, at : at + width] for i in range(count)]


def masked(scal, step, steps, mid):
    width = mid.shape[0]
    weight = scal[1 + 3 * steps + step].astype(F32)
    a_rank, b_rank = scal[1 + steps + step], scal[1 + 2 * steps + step]
    return mid * rows_below(a_rank, width, width) * lanes_below(b_rank, width, width) * weight


def first_kernel(steps, scal, ar, probe, *refs):
    (x, x1, x2, l3, r3), (core, cross, mid_out, rp_out, k_out, y_out, gram_out) = refs[:5], refs[5:]
    width = mid_out.shape[0]
    tmask = lanes_below(scal[1], width, width)
    k_out[:width, :] = core[0] * rows_below(scal[0], width, width) * tmask
    b_left, b_right = pieces_of([x.at[0], x1.at[0], x2.at[0], l3]), pieces_of([x.at[1], x1.at[1], x2.at[1], r3])
    mid = masked(scal, 0, steps, summed(split_rows(ar, 4, 0, width), b_left))
    mid_out[...] = mid
    rp = summed(b_right, split_rows(probe, 4, 0, steps * width))
    rp_out[...] = rp[:, width:]
    k_out[width:, :] = exact(mid, rp[:, :width] * tmask)
    k = k_out[...]
    y = exact(cross[: 2 * width, : 2 * width], k)
    y_out[...] = y
    gram_out[...] = exact_at(k, y) + unit_beyond(scal[1], width)


def early_kernel(tile, scal, gram, k0, y0, cross, mid0, rp01, core, work_out, t_out):
    width = gram.shape[0]
    root = math.sqrt(tile)
    work_out[...] = gram[...]

    def next_core():
        y = jnp.concatenate([y0[:width, :] * rows_below(scal[0], width, width), y0[width:, :]], 0)
        z = jnp.concatenate([core[1], exact(mid0[...], rp01[...])], 0)
        t_out[:, :width] = exact_at(y, z) * (1.0 / root)

    def next_cross():
        t_out[:, width:] = exact(cross[2 * width :, : 2 * width], k0[...]).T * root

    inverse_factor(work_out, [next_core, next_cross], 0, width // PANEL // 2)


def late_kernel(masks_a, steps, scal, work, t, k0, y0, mid0, ar, probe, x, x1, x2, left, *refs):
    n = len(masks_a)
    al, (core_out, h_out, h_a_out, mid_out, rp_out, k_out, back_out, s_out) = refs[:n], refs[n : n + 8]
    work_v, left_v, a_v, sems = refs[n + 8 :]
    tile, width = left_v.shape
    root = math.sqrt(tile)
    late = place([r.at[:, 0] for r in al], masks_a, scal[1 + 4 * steps], a_v, sems, 0)
    late.append(pltpu.make_async_copy(left, left_v, sems.at[n]))
    work_v[...] = work[...]

    def fetch():
        for copy in late:
            copy.start()

    def middle_part():
        mid_out[...] = summed(split_rows(ar, 4, width, width)[:3], pieces_of([r.at[0] for r in (x, x1, x2)]))

    def probe_part():
        rp_out[...] = summed(pieces_of([r.at[1] for r in (x, x1, x2)]), split_rows(probe, 4, width, width)[:3])

    inverse_factor(work_v, [fetch, middle_part, probe_part], width // PANEL // 2)
    w = work_v[...]
    both = exact(w, t[...])
    keep = rows_below(scal[1], width, width)
    a = both[:, :width] * keep * lanes_below(scal[2], width, width)
    h = both[:, width:] * keep
    core_out[...] = a
    h_out[...] = h
    h_a_out[...] = exact_at(h, a)
    k_c = close(k0[...], close_at(w, a) * root)
    k_out[...] = k_c
    z = close_bt(y0[...], w)
    back_out[:width, :] = z[:width] * rows_below(scal[0], width, width)
    back_out[width:, :] = close_at(mid0[...], z[width:])
    k_h, k_m = split2(k_c)
    weights = jnp.concatenate([k_h[:width], k_h[:width], k_m[:width], k_h[width:], k_m[width:]], 0)
    for copy in late:
        copy.wait()
    for c in range(tile // CHUNK):
        at = slice(c * CHUNK, (c + 1) * CHUNK)
        l_h, l_m = split2(left_v[at, :])
        o = a_v[at, :]
        s_out[at, :] = mm(jnp.concatenate([l_h, l_m, l_h, o, o], 1), weights)


def second_kernel(
    masks_a, masks_b, steps, scal, core_c, h0, h_a, mid_part, rp_part, k_c, back0, s_part, cross, ar, probe,
    l3, r3, right, b0, b1, b2, br3, p0, p1, p2, pr3, *refs,
):
    n = len(masks_a)
    al, (out_left, out_right), refs = refs[:n], refs[n : n + 2], refs[n + 2 :]
    right_v, a_v, b_v, gram_v, k_v, q_v, outl_v, outr_v, sems, out_sems = refs
    tile, width = right_v.shape
    root = math.sqrt(tile)
    col_at, row_at = scal[1 + 4 * steps], scal[2 + 4 * steps]
    late = place([r.at[:, 1] for r in al], masks_a, col_at, a_v, sems, 0)
    for k, (x, x1, x2, x3) in enumerate(((p0, p1, p2, pr3), (b0, b1, b2, br3))):
        here = pl.ds(k * width, width)
        late += place((x.at[1], x1.at[1], x2.at[1], x3), masks_b, row_at, b_v.at[:, here], sems, len(late))
    late.append(pltpu.make_async_copy(right, right_v, sems.at[len(late)]))
    t0, t1 = scal[1], scal[2]
    a = core_c[...]
    h = h0[...]
    mid1 = masked(scal, 1, steps, mid_part[...] + summed(split_rows(ar, 4, width, width)[3:], pieces_of([l3])))
    rp11 = rp_part[...] + summed(pieces_of([r3]), split_rows(probe, 4, width, width)[3:])
    core_b = exact(mid1, rp11 * lanes_below(t1, width, width))
    both = exact(jnp.concatenate([h, cross[2 * width :, 2 * width :]], 0), core_b)
    top = a * float(tile) + both[:width]
    low = h_a[...] + both[width:]
    gram_v[...] = exact_at(jnp.concatenate([a, core_b], 0), jnp.concatenate([top, low], 0)) + unit_beyond(t1, width)

    def left_weights():
        k_v[...] = jnp.concatenate(split2(core_b), 0)

    def right_weights():
        q_c = close(back0[...], top * rows_below(t0, width, width)) * (1.0 / tile)
        h, m = split2(jnp.concatenate([q_c, close_at(mid1, low) * (1.0 / root)], 0))
        q_v[...] = jnp.concatenate([h[:width], h[:width], m[:width], h[width:], m[width:]], 0)

    def fetch():
        for copy in late:
            copy.start()

    def arrive():
        for copy in late:
            copy.wait()

    def form_left(c):
        at = slice(c * CHUNK, (c + 1) * CHUNK)
        o = a_v[at, :]
        outl_v[at, :] = s_part[at, :] + mm(jnp.concatenate([o, o], 1), k_v[...])

    def form_right(c):
        at = slice(c * CHUNK, (c + 1) * CHUNK)
        h, m = split2(right_v[at, :])
        o = b_v[at, :]
        outr_v[at, :] = mm(jnp.concatenate([h, m, h, o, o], 1), q_v[...])

    count = tile // CHUNK
    beside = [fetch, left_weights, right_weights, arrive]
    for form in (form_left, form_right):
        beside += [functools.partial(form, c) for c in range(count)]
    inverse_factor(gram_v, beside)
    h, m = split2(gram_v[...])
    weights = jnp.concatenate([h, h, m], 1)
    outs = []
    for c in range(count):
        at = pl.ds(c * CHUNK, CHUNK)
        for src, dst, scale in ((outl_v, out_left, root), (outr_v, out_right, 1.0)):
            h, m = split2(src[at, :])
            src[at, :] = mm_bt(jnp.concatenate([h, m, h], 1), weights) * scale
            copy = pltpu.make_async_copy(src.at[at, :], dst.at[at, :], out_sems.at[len(outs)])
            copy.start()
            outs.append(copy)
    for copy in outs:
        copy.wait()


def call(kernel, out_shape, in_specs, scratch, name, vmem, passes, out_space=VMEM):
    flops = passes * 2 * 2048 * 256 * 256
    return pl.pallas_call(
        kernel,
        out_shape=out_shape,
        in_specs=in_specs,
        out_specs=jax.tree.map(lambda _: pl.BlockSpec(memory_space=out_space), out_shape),
        scratch_shapes=scratch,
        compiler_params=pltpu.CompilerParams(vmem_limit_bytes=vmem * 1024 * 1024),
        cost_estimate=pl.CostEstimate(flops=flops, bytes_accessed=1 << 20, transcendentals=0),
        name=name,
    )


def on_device(
    rows_count, cols_count, c_left, c_right, c_rank, a_left, a_right, a_rank, a_pattern,
    b_left, b_right, b_rank, b_pattern, probe, target,
):
    tile, width = c_left.shape[2:]
    steps = probe.shape[0]
    left = c_left[0, 0]
    right = c_right[0, 0]
    any_, vm, sm = (pl.BlockSpec(memory_space=s) for s in (ANY, VMEM, SMEM))
    dma = pltpu.SemaphoreType.DMA

    def f32(*shape):
        return jax.ShapeDtypeStruct(shape, F32)

    scal = jnp.concatenate(
        [
            c_rank[0],
            target[0, 0],
            a_rank[0],
            b_rank[:, 0],
            a_pattern[0] * b_pattern[:, 0],
            jnp.stack([lax.axis_index("col"), lax.axis_index("row")]),
        ]
    ).astype(jnp.int32)

    whole = VMEM((tile, width), F32)
    wide = VMEM((tile, steps * width), BF16)
    a_bits = bits_of(cols_count)
    al, masks = spread(a_left, "col", cols_count, a_bits)
    ar, _ = spread(a_right, "col", cols_count, a_bits)
    masks_a = [[mask] for mask in masks]
    bits = bits_of(rows_count)
    one, two = bits[-1], bits[-2]
    core = call(
        functools.partial(probe_kernel, steps),
        f32(steps, width, width),
        [any_, any_],
        [VMEM((tile, width), F32), VMEM((tile, steps * width), BF16), dma((1 + steps,))],
        "right_probe",
        16,
        12,
    )(right, probe)
    cross = call(
        functools.partial(cross_kernel, masks_a, steps),
        f32((1 + steps) * width, (1 + steps) * width),
        [sm] + [any_] * (1 + cols_count),
        [VMEM((tile, width), F32), VMEM((tile, (2 + steps) * width), BF16), dma((1 + steps * cols_count,))],
        "left_cross",
        24,
        24,
    )(scal, left, *al)

    def own_blocks(k, *before):
        x = jnp.stack([b_left[k, 0], b_right[k, 0]])[:, None]
        return (forwarded if True else spread)(after(x, *before) if before else x, "row", rows_count, bits[:-2])

    blocks, masks = own_blocks(0)
    masks_b = [[mask ^ flip for mask in masks] for flip in (0, one, two, one ^ two)]
    ordered = call(
        functools.partial(order_kernel, masks_a, masks_b, steps),
        (jax.ShapeDtypeStruct((tile, steps * width), BF16),) * 2,
        [sm] + [any_] * (1 + cols_count),
        [wide, wide, dma((steps * (cols_count + 1),))],
        "ordered",
        20,
        5,
    )(scal, probe, *ar)
    gathered = []
    for k in range(steps):
        x = jnp.concatenate(blocks, 1)
        x = after(x, *gathered[k - 1][3:]) if k > 0 else after(x, core, al[-1])
        x1 = exchange(x, "row", rows_count, one)
        x2 = exchange(x, "row", rows_count, two)
        before = ()
        if k == 0:
            blocks, _ = own_blocks(1, x)
            before = (cross, *ordered)
        l3 = exchange(after(x1[0], *before), "row", rows_count, two)
        r3 = exchange(after(x2[1], *before), "row", rows_count, one)
        gathered.append((x, x1, x2, l3, r3))

    mid0, rp01, k0, y0, gram = call(
        functools.partial(first_kernel, steps),
        (f32(width, width), f32(width, width), f32(2 * width, width), f32(2 * width, width), f32(width, width)),
        [sm] + [vm] * 9,
        [],
        "first_step",
        20,
        20,
    )(scal, *ordered, *gathered[0], core, cross)
    square = f32(width, width)
    work, t = call(
        functools.partial(early_kernel, tile),
        (square, f32(width, 2 * width)),
        [sm] + [vm] * 7,
        [],
        "factor_early",
        20,
        15,
    )(scal, gram, k0, y0, cross, mid0, rp01, core)
    x, x1, x2, l3, r3 = gathered[1]
    tall = f32(2 * width, width)
    state = call(
        functools.partial(late_kernel, masks_a, steps),
        (square, square, square, square, square, tall, tall, f32(tile, width)),
        [sm] + [vm] * 10 + [any_] * (1 + cols_count),
        [VMEM((width, width), F32), whole, VMEM((tile, width), BF16), dma((cols_count + 1,))],
        "factor_late",
        24,
        25,
    )(scal, work, t, k0, y0, mid0, *ordered, x, x1, x2, left, *al)
    out_left, out_right = call(
        functools.partial(second_kernel, masks_a, masks_b, steps),
        (f32(tile, width), f32(tile, width)),
        [sm] + [vm] * 13 + [any_] * (9 + cols_count),
        [
            whole, VMEM((tile, width), BF16), wide, VMEM((width, width), F32),
            VMEM((2 * width, width), BF16), VMEM(((3 + 2 * steps) * width, width), BF16), whole, whole,
            dma((2 * rows_count + cols_count + 1,)), dma((2 * (tile // CHUNK),)),
        ],
        "second_step",
        36,
        100,
        ANY,
    )(
        scal, *state, cross, *ordered, l3, r3, right, x, x1, x2, r3, *[gathered[0][i] for i in (0, 1, 2, 4)], *al
    )
    return (out_left[None, None], out_right[None, None])


def solution(mesh):
    return jax.shard_map(
        functools.partial(on_device, mesh.shape["row"], mesh.shape["col"]),
        mesh=mesh,
        in_specs=(
            P("row", "col", None, None),
            P("row", "col", None, None),
            P("row", "col"),
            P("row", None, "col", None),
            P("row", None, "col", None),
            P("row", None),
            P("row", None),
            P(None, "col", "row", None),
            P(None, "col", "row", None),
            P(None, "col"),
            P(None, "col"),
            P(),
            P("row", "col", None),
        ),
        out_specs=(P("row", "col", None, None), P("row", "col", None, None)),
        check_vma=False,
    )
```
